512 devices in a mesh: seq: 128 (over z, y, core), tp: 4 (over x).
Axes of the slice: x: 4, y: 8, z: 8, core: 2. Of those that a mesh axis runs over, the one named last changes fastest.
Arguments:
- queries: bfloat16 [16384, 4096], P('seq', 'tp'), may hold values from -128 to 128
- keys: bfloat16 [16384, 4096], P('seq', 'tp'), may hold values from -6 to 6
- values: bfloat16 [16384, 4096], P('seq', 'tp'), may hold values from -18 to 18
- residual_in: bfloat16 [16384, 4096], P('seq', 'tp'), may hold values from -6 to 6
- norm_gain: float32 [4096], replicated, may hold values from 0.1 to 1.9
- routing: int32 [128, 1], replicated, may hold values from 0 to 63; in each aligned block of 128 rows (0 to 127, 128 to 255, ...) at most 4 rows name the same one
- gate_weight: bfloat16 [128, 4096, 512], P('seq', None, 'tp'), may hold values from -0.09375 to 0.09375
- up_weight: bfloat16 [128, 4096, 512], P('seq', None, 'tp'), may hold values from -0.09375 to 0.09375
- down_weight: bfloat16 [128, 512, 4096], P('seq', None, 'tp'), may hold values from -0.1875 to 0.1875
Outputs:
- mixed: bfloat16 [16384, 4096], P('seq', 'tp')
The draws below stay inside these ranges and needn't reach their ends.
Inputs may be any that keep to these rules, and one draw needn't show every extreme that they name: `routing`: every expert is named by some block; no expert by more than 4 blocks, and one by exactly 4.
All inputs are finite; a program needn't handle non-finite values.
Results may differ from the reference program's by a relative error of at most 0.006.
Values may be sent and summed in bfloat16 or wider, within the bound.
No kernel may reach another device: no remote copies, remote signals or barrier semaphores. Data moves between devices by JAX's collectives and lax.ppermute only.
A program may use at most 64 MiB of HBM per device.

```python
import math
import jax
import jax.numpy as jnp
import numpy as np
from jax import lax

HEADS = 32
HEAD_DIM = 128
FF = 1024
BLOCK = 128
WINDOW = 512
D = 4096
TOKENS = 16384
NBLOCKS = 128
EXPERTS = 64
MOST = 4


def raw_keys(key):
    return jnp.clip(jax.random.normal(jax.random.fold_in(key, 11), (TOKENS, D), jnp.float32), -6.0, 6.0)


def draw_keys(key, part):
    base_keys = raw_keys(key)
    return base_keys.astype(jnp.bfloat16)


def draw_queries(key, part):
    drawn = jnp.clip(jax.random.normal(jax.random.fold_in(key, 12), (TOKENS, D), jnp.float32), -6.0, 6.0)
    return drawn.astype(jnp.bfloat16)


def shard_levels(own_key, dims, cuts, least, largest):
    level = 1.0
    for axis_at, blocks in cuts:
        heights = jax.random.uniform(jax.random.fold_in(jax.random.fold_in(own_key, 6), axis_at), (blocks,), jnp.float32, least / len(cuts), largest / len(cuts))
        level = level * jnp.repeat(jnp.exp(heights), dims[axis_at] // blocks).reshape((-1,) + (1,) * (len(dims) - 1 - axis_at))
    return level


def assign_block(stream_key, own, number, rows, count, top, bound, slope):
    sequence = jax.random.permutation(stream_key, count)
    packed, common = load_shares(count, rows * top, bound, slope, True), load_shares(count, rows * top, bound, slope, False)
    places = jnp.arange(count)

    def named(tallies, rotation):
        used = int((tallies > 0).sum())
        fixed = max(1, used // 4)
        moved = fixed + (places - fixed + rotation * (used - fixed)) % max(1, count - fixed)
        return jnp.zeros((count,), jnp.int32).at[sequence[jnp.where(places < fixed, places, moved)]].set(jnp.asarray(tallies, jnp.int32))

    tallies = jnp.where(number % 4 == 0, named(packed, number // 4), named(common, number - number // 4 - 1))
    mixed = jax.random.permutation(jax.random.fold_in(own, 3), count)
    source_of, receiver = mixed[0:count // 2 * 2:2], mixed[1:count // 2 * 2:2]
    margin = jnp.minimum(tallies[source_of] - 1, bound - tallies[receiver]) // 2
    margin = jnp.where((source_of == sequence[0]) | (receiver == sequence[0]) | (tallies[receiver] == 0), 0, jnp.maximum(margin, 0))
    moved = jax.random.randint(jax.random.fold_in(own, 4), (count // 2,), 0, 1 << 20) % (margin + 1)
    tallies = tallies.at[source_of].add(-moved).at[receiver].add(moved)
    labels = jnp.searchsorted(jnp.cumsum(tallies), jnp.arange(rows * top), side="right").astype(jnp.int32)
    listing = labels.reshape(top, rows).T
    listing = listing[jax.random.permutation(jax.random.fold_in(own, 1), rows)]
    rotation = jax.random.randint(jax.random.fold_in(own, 2), (rows, 1), 0, top)
    return jnp.take_along_axis(listing, (jnp.arange(top)[None, :] + rotation) % top, axis=1)


def load_shares(number_of, total, limit, lean, full):
    portions = [(1 << 20) // math.isqrt(grade ** lean) + 1 for grade in range(1, number_of + 1)]
    largest = limit if full else min(limit, max(-(-total // number_of), total * portions[0] // sum(portions)))
    least = 1 if total - largest >= number_of - 1 else 0
    holding, spare = [largest] + [least] * (number_of - 1), total - largest - least * (number_of - 1)
    while spare > 0:
        movable = [i for i in range(1, number_of) if holding[i] < largest] or [i for i in range(1, number_of) if holding[i] < limit]
        whole, left = sum([portions[i] for i in movable]), spare
        for i in movable:
            more = min(limit - holding[i], max(1, left * portions[i] // whole), spare)
            holding[i] = holding[i] + more
            spare = spare - more
    return np.array(holding)


def scatter_about(key, shape, deviation, most, shards=(), kind=jnp.bfloat16):
    factor_of = shard_levels(key, shape, shards, -0.22, 0.18) if shards else 1.0
    entries = jax.random.normal(key, shape, jnp.float32) * deviation * factor_of
    return jnp.minimum(jnp.maximum(entries, -most), most).astype(kind)


def setup_inputs(seed: int = 0) -> dict:
    arg_keys = jax.random.split(jax.random.key(seed), 10)
    queries = draw_queries(jax.random.fold_in(arg_keys[9], 71), 0)
    keys = draw_keys(jax.random.fold_in(arg_keys[9], 71), 0)
    values = scatter_about(arg_keys[2], (TOKENS, D), 3.0, 18.0, ((0, 128), (1, 4)))
    residual_in = scatter_about(arg_keys[3], (TOKENS, D), 1.0, 6.0, ((0, 128), (1, 4)))
    norm_gain = jnp.clip(1.0 + 0.18 * jax.random.normal(arg_keys[4], (D,), jnp.float32), 0.1, 1.9)
    routing_keys = jax.random.split(jax.random.fold_in(arg_keys[5], 1), NBLOCKS // NBLOCKS)
    routing_turns = jax.random.permutation(jax.random.fold_in(arg_keys[5], 3), NBLOCKS // NBLOCKS)
    routing = jax.vmap(lambda own, number: assign_block(jax.random.fold_in(arg_keys[5], 2), own, number, NBLOCKS, EXPERTS, 1, MOST, 2))(routing_keys, routing_turns).reshape((NBLOCKS, 1))
    gate_weight = scatter_about(arg_keys[6], (2 * EXPERTS, D, FF // 2), D ** -0.5, 0.09375, ((0, 128), (2, 4)))
    up_weight = scatter_about(arg_keys[7], (2 * EXPERTS, D, FF // 2), D ** -0.5, 0.09375, ((0, 128), (2, 4)))
    down_weight = scatter_about(arg_keys[8], (2 * EXPERTS, FF // 2, D), FF ** -0.5, 0.1875, ((0, 128), (2, 4)))
    return dict(queries=queries, keys=keys, values=values, residual_in=residual_in, norm_gain=norm_gain, routing=routing, gate_weight=gate_weight, up_weight=up_weight, down_weight=down_weight)


epsilon = 1e-05
masked_score = -1e+30

def attend_block(block_index, query_heads, key_padded, value_padded):
    begin_row = block_index * BLOCK
    query_block = lax.dynamic_slice_in_dim(query_heads, begin_row, BLOCK, 0).astype(jnp.float32)
    key_block = lax.dynamic_slice_in_dim(key_padded, begin_row, WINDOW + BLOCK, 0).astype(jnp.float32)
    value_block = lax.dynamic_slice_in_dim(value_padded, begin_row, WINDOW + BLOCK, 0).astype(jnp.float32)
    query_pos = begin_row + jnp.arange(BLOCK, dtype=jnp.int32)
    key_pos = begin_row - WINDOW + jnp.arange(WINDOW + BLOCK, dtype=jnp.int32)
    visible = (key_pos[None, :] >= 0) & (key_pos[None, :] <= query_pos[:, None]) & (key_pos[None, :] > query_pos[:, None] - WINDOW)
    scores = jnp.einsum('qhd,khd->hqk', query_block, key_block) * (1.0 / math.sqrt(HEAD_DIM))
    scores = jnp.where(visible[None], scores, masked_score)
    top_score = lax.optimization_barrier(jnp.max(scores, axis=2, keepdims=True))
    expo = jnp.exp(scores - top_score)
    weights_soft = (expo / lax.optimization_barrier(jnp.sum(expo, axis=2, keepdims=True))).astype(jnp.bfloat16)
    attended = jnp.einsum('hqk,khd->qhd', weights_soft.astype(jnp.float32), value_block)
    return attended.reshape(BLOCK, D)

def expert_block(stream_block, expert, norm_gain, gate_weight, up_weight, down_weight):
    stream_f32 = stream_block.astype(jnp.float32)
    mean_square = lax.optimization_barrier(jnp.mean(stream_f32 * stream_f32, axis=1, keepdims=True))
    normed = (stream_f32 * lax.rsqrt(mean_square + epsilon) * norm_gain).astype(jnp.bfloat16)
    summed = stream_f32
    for half_index in range(2):
        weight_row = (2 * expert + half_index).astype(jnp.int32)
        gate_rows = lax.dynamic_index_in_dim(gate_weight, weight_row, 0, keepdims=False)
        up_rows = lax.dynamic_index_in_dim(up_weight, weight_row, 0, keepdims=False)
        down_rows = lax.dynamic_index_in_dim(down_weight, weight_row, 0, keepdims=False)
        gate_val = jnp.dot(normed, gate_rows, preferred_element_type=jnp.float32)
        up_val = jnp.dot(normed, up_rows, preferred_element_type=jnp.float32)
        hidden = (jax.nn.silu(gate_val) * up_val).astype(jnp.bfloat16)
        branch = jnp.dot(hidden, down_rows, preferred_element_type=jnp.float32).astype(jnp.bfloat16)
        summed = summed + branch.astype(jnp.float32)
    return summed.astype(jnp.bfloat16)

def reference(queries, keys, values, residual_in, norm_gain, routing, gate_weight, up_weight, down_weight):
    query_heads = queries.reshape(TOKENS, HEADS, HEAD_DIM)
    zero_rows = jnp.zeros((WINDOW, D), keys.dtype)
    key_padded = jnp.concatenate([zero_rows, keys], axis=0).reshape(WINDOW + TOKENS, HEADS, HEAD_DIM)
    value_padded = jnp.concatenate([zero_rows, values], axis=0).reshape(WINDOW + TOKENS, HEADS, HEAD_DIM)
    attended = lax.map(lambda index: attend_block(index, query_heads, key_padded, value_padded), jnp.arange(NBLOCKS, dtype=jnp.int32))
    stream = (residual_in.reshape(NBLOCKS, BLOCK, D).astype(jnp.float32) + attended).astype(jnp.bfloat16)
    mixed = lax.map(lambda pair: expert_block(pair[0], pair[1], norm_gain, gate_weight, up_weight, down_weight), (stream, routing[:, 0]))
    return mixed.reshape(TOKENS, D)
```

```python
import math

import jax
import jax.numpy as jnp
from jax import lax
from jax.experimental import pallas as pl
from jax.experimental.pallas import tpu as pltpu
from jax.sharding import PartitionSpec as P

HEAD_DIM = 128
BLOCK = 128
WINDOW = 512
TILE = 8

epsilon = 1e-05
masked_score = -1e30
f32 = jnp.float32
bf16 = jnp.bfloat16

VMEM_LIMIT = 40 * 1024 * 1024


def params():
    return pltpu.CompilerParams(vmem_limit_bytes=VMEM_LIMIT)


def vmem():
    return pl.BlockSpec(memory_space=pltpu.VMEM)


def smem():
    return pl.BlockSpec(memory_space=pltpu.SMEM)


def dot(a, b):
    return lax.dot_general(a, b, (((1,), (0,)), ((), ())), preferred_element_type=f32)


def dot_t(a, b):
    return lax.dot_general(a, b, (((1,), (1,)), ((), ())), preferred_element_type=f32)


def attend_kernel(
    place, q, k0, k1, k2, kx0, kx1, kx2, v0, v1, v2, vx0, vx1, vx2, res, out
):
    chip = place[0]
    core = place[1]
    row = lax.broadcasted_iota(jnp.int32, (BLOCK, BLOCK), 0)
    col = lax.broadcasted_iota(jnp.int32, (BLOCK, BLOCK), 1)
    big = jnp.int32(4 * BLOCK)
    shift1 = jnp.where(chip >= 1, 0, big)
    shift2 = jnp.where(chip >= 2, 0, big)
    shiftx = jnp.where((chip >= 2) | (core == 1), 0, big)
    diff = col - row
    visible = jnp.concatenate(
        [
            diff > shift2,
            diff + BLOCK > shiftx,
            diff + BLOCK > shift1,
            diff + BLOCK > shift1,
            diff <= 0,
        ],
        axis=1,
    )
    heads = q.shape[1] // HEAD_DIM
    for h in range(heads):
        s = slice(h * HEAD_DIM, (h + 1) * HEAD_DIM)
        key_all = jnp.concatenate(
            [k2[:, s], kx0[:, s] + kx2[:, s], k1[:, s], kx1[:, s], k0[:, s]], axis=0
        )
        value_all = jnp.concatenate(
            [v2[:, s], vx0[:, s] + vx2[:, s], v1[:, s], vx1[:, s], v0[:, s]], axis=0
        )
        scores = dot_t(q[:, s], key_all) * (1.0 / math.sqrt(HEAD_DIM))
        scores = jnp.where(visible, scores, masked_score)
        top = jnp.max(scores, axis=1, keepdims=True)
        expo = jnp.exp(scores - top)
        weights = (expo * (1.0 / jnp.sum(expo, axis=1, keepdims=True))).astype(bf16)
        attended = dot(weights, value_all)
        stream = res[:, s].astype(f32) + attended
        z_count, core_count = out.shape[0], out.shape[2]
        out[:, h] = stream.reshape(z_count, core_count, TILE, HEAD_DIM).astype(bf16)


def pick_kernel(index, tiles, out):
    @pl.loop(0, out.shape[0], unroll=8)
    def _(i):
        out[i] = tiles[index[i]]


def project_kernel(tiles, gain, gate0, gate1, up0, up1, out, held):
    z_count, heads, slots = tiles.shape[:3]
    rows = z_count * slots * TILE
    squares = jnp.zeros((rows, HEAD_DIM), f32)
    for h in range(heads):
        value = tiles[:, h].astype(f32).reshape(rows, HEAD_DIM)
        squares = squares + value * value
        s = slice(h * HEAD_DIM, (h + 1) * HEAD_DIM)
        held[:, s] = (value * gain[:, s]).astype(bf16)
    high = squares.astype(bf16)
    low = (squares - high.astype(f32)).astype(bf16)
    ones = jnp.ones((TILE, HEAD_DIM), bf16)
    total = dot_t(ones, high) + dot_t(ones, low)
    total_high = total.astype(bf16).astype(f32)
    total_rows = jnp.concatenate([total_high, total - total_high], axis=0).astype(bf16)
    x = held[...]
    parts = out.shape[0]
    for t in range(parts):
        gate = dot(x, jnp.concatenate([gate0[t], gate1[t]], axis=1))
        up = dot(x, jnp.concatenate([up0[t], up1[t]], axis=1))
        width = gate.shape[1]
        out[t, :rows, :width] = gate.astype(bf16)
        out[t, :rows, width:] = up.astype(bf16)
        out[t, rows:, :rows] = total_rows
        out[t, rows:, rows:] = total_rows


def hidden_kernel(features, parts, out):
    count = parts.shape[0]
    rows, width = out.shape
    tail = parts.shape[1] - rows
    sums = parts[:, rows:, :rows].reshape(count * tail, rows)
    weight = jnp.full((count * tail, HEAD_DIM), 1.0 / TILE, bf16)
    square = lax.dot_general(
        sums, weight, (((0,), (0,)), ((), ())), preferred_element_type=f32
    )
    factor = lax.rsqrt(square * (1.0 / features) + epsilon)
    for s in range(0, width, HEAD_DIM):
        gate = sum(parts[t, :rows, s : s + HEAD_DIM].astype(f32) for t in range(count))
        up = sum(
            parts[t, :rows, width + s : width + s + HEAD_DIM].astype(f32) for t in range(count)
        )
        gate = gate * factor
        up = up * factor
        out[:, s : s + HEAD_DIM] = (gate / (1.0 + jnp.exp(-gate)) * up).astype(bf16)


def branch_kernel(hidden, down0, down1, out):
    count = hidden.shape[0]
    half = hidden.shape[2] // 2
    first = jnp.concatenate([hidden[t, :, :half] for t in range(count)], axis=1)
    second = jnp.concatenate([hidden[t, :, half:] for t in range(count)], axis=1)
    z_count, heads, slots = out.shape[:3]
    step = 2 * HEAD_DIM
    for s in range(0, heads * HEAD_DIM, step):
        value = dot(first, down0[:, s : s + step]) + dot(second, down1[:, s : s + step])
        for k in range(0, step, HEAD_DIM):
            part = value[:, k : k + HEAD_DIM].reshape(z_count, slots, TILE, HEAD_DIM)
            out[:, (s + k) // HEAD_DIM] = part.astype(bf16)


def finish_kernel(stream, branch, out):
    z_count, heads, cores = stream.shape[:3]
    for h in range(heads):
        value = stream[:, h].astype(f32) + branch[:, h].astype(f32)
        out[:, h * HEAD_DIM : (h + 1) * HEAD_DIM] = value.reshape(
            z_count * cores * TILE, HEAD_DIM
        ).astype(bf16)


def local(
    queries, keys, values, residual_in, norm_gain, routing, gate_weight, up_weight, down_weight
):
    seq_count = lax.axis_size("seq")
    tp_count = lax.axis_size("tp")
    seq_place = lax.axis_index("seq")
    tp_place = lax.axis_index("tp")
    chips = seq_count // 2
    rows, width = queries.shape
    heads = width // HEAD_DIM
    z_count = rows // (2 * TILE)
    slots = 4

    onward = [(i, i + 2) for i in range(seq_count - 2)]
    to_odd = [(i, i + 1) for i in range(0, seq_count, 2)]
    to_even = [(i + 1, i) for i in range(0, seq_count, 2)]
    swap = to_odd + to_even
    same_core = [[c + 2 * i for i in range(chips)] for c in (0, 1)]

    def move(x, route):
        return lax.ppermute(x, "seq", route)

    k1 = move(keys, onward)
    v1 = move(values, onward)
    k2 = move(k1, onward)
    v2 = move(v1, onward)
    kx0 = move(keys, to_odd)
    vx0 = move(values, to_odd)
    kx1 = move(k1, swap)
    vx1 = move(v1, swap)
    kx2 = move(k2, to_even)
    vx2 = move(v2, to_even)

    def by_features(w):
        w = w[0].reshape(tp_count, width, w.shape[2])
        return lax.all_to_all(w, "tp", 0, 0, tiled=True)

    gate0 = by_features(gate_weight)
    up0 = by_features(up_weight)
    down0 = down_weight[0]
    gate1 = move(gate0, swap)
    up1 = move(up0, swap)
    down1 = move(down0, swap)
    gain = lax.dynamic_slice_in_dim(norm_gain, tp_place * width, width)[None]

    expert = routing[:, 0]
    block_range = jnp.arange(seq_count, dtype=jnp.int32)
    same = expert[None, :] == expert[:, None]
    rank = jnp.sum(same & (block_range[None, :] < block_range[:, None]), axis=1, dtype=jnp.int32)
    slot_of = expert * slots + rank
    slot_range = jnp.arange(chips * slots, dtype=jnp.int32)
    block_of = jnp.sum(
        jnp.where(slot_range[:, None] == slot_of[None, :], block_range[None, :], 0),
        axis=1,
        dtype=jnp.int32,
    )
    place = jnp.stack([seq_place // 2, seq_place % 2]).astype(jnp.int32)

    stream = pl.pallas_call(
        attend_kernel,
        out_shape=jax.ShapeDtypeStruct((z_count, heads, 2, TILE, HEAD_DIM), bf16),
        in_specs=[smem()] + [vmem()] * 14,
        out_specs=vmem(),
        compiler_params=params(),
        name="attend",
    )(place, queries, keys, k1, k2, kx0, kx1, kx2, values, v1, v2, vx0, vx1, vx2, residual_in)

    tiles = lax.all_to_all(
        stream.reshape(seq_count, TILE, HEAD_DIM), "seq", 0, 0, tiled=True
    )

    def pick(index, source):
        return pl.pallas_call(
            pick_kernel,
            out_shape=jax.ShapeDtypeStruct((index.shape[0], TILE, HEAD_DIM), bf16),
            in_specs=[smem(), vmem()],
            out_specs=vmem(),
            compiler_params=params(),
            name="pick",
        )(index, source)

    def same_core_exchange(x):
        x = x.reshape(chips, slots, TILE, HEAD_DIM)
        return lax.all_to_all(x, "seq", 0, 0, tiled=True, axis_index_groups=same_core)

    arrived = same_core_exchange(pick(block_of, tiles))
    arrived = arrived.reshape(z_count, heads, slots, TILE, HEAD_DIM)
    work = z_count * slots * TILE
    hid = 2 * gate0.shape[2]
    parts = pl.pallas_call(
        project_kernel,
        out_shape=jax.ShapeDtypeStruct((tp_count, work + 2 * TILE, 2 * hid), bf16),
        in_specs=[vmem()] * 6,
        out_specs=vmem(),
        scratch_shapes=[pltpu.VMEM((work, width), bf16)],
        compiler_params=params(),
        name="project",
    )(arrived, gain, gate0, gate1, up0, up1)
    parts = lax.all_to_all(parts, "tp", 0, 0, tiled=True)

    def run_hidden(parts_ref, out_ref):
        hidden_kernel(width * tp_count, parts_ref, out_ref)

    hidden = pl.pallas_call(
        run_hidden,
        out_shape=jax.ShapeDtypeStruct((work, hid), bf16),
        in_specs=[vmem()],
        out_specs=vmem(),
        compiler_params=params(),
        name="hidden",
    )(parts)
    hidden = lax.all_gather(hidden, "tp")
    branch = pl.pallas_call(
        branch_kernel,
        out_shape=jax.ShapeDtypeStruct((z_count, heads, slots, TILE, HEAD_DIM), bf16),
        in_specs=[vmem()] * 3,
        out_specs=vmem(),
        compiler_params=params(),
        name="branch",
    )(hidden, down0, down1)
    returned = same_core_exchange(branch).reshape(chips * slots, TILE, HEAD_DIM)
    finished = lax.all_to_all(pick(slot_of, returned), "seq", 0, 0, tiled=True)
    return pl.pallas_call(
        finish_kernel,
        out_shape=jax.ShapeDtypeStruct((rows, width), bf16),
        in_specs=[vmem()] * 2,
        out_specs=vmem(),
        compiler_params=params(),
        name="finish",
    )(stream, finished.reshape(stream.shape))


def solution(mesh):
    in_specs = (
        P("seq", "tp"),
        P("seq", "tp"),
        P("seq", "tp"),
        P("seq", "tp"),
        P(),
        P(),
        P("seq", None, "tp"),
        P("seq", None, "tp"),
        P("seq", None, "tp"),
    )
    out_specs = P("seq", "tp")
    return jax.shard_map(local, mesh=mesh, in_specs=in_specs, out_specs=out_specs, check_vma=False)
```

```python
import math

import jax
import jax.numpy as jnp
from jax import lax
from jax.experimental import pallas as pl
from jax.experimental.pallas import tpu as pltpu
from jax.sharding import PartitionSpec as P

HEAD_DIM = 128
BLOCK = 128
WINDOW = 512
TILE = 8

epsilon = 1e-05
masked_score = -1e30
f32 = jnp.float32
bf16 = jnp.bfloat16

VMEM_LIMIT = 14 * 1024 * 1024


def params():
    return pltpu.CompilerParams(vmem_limit_bytes=VMEM_LIMIT)


def vmem():
    return pl.BlockSpec(memory_space=pltpu.VMEM)


def smem():
    return pl.BlockSpec(memory_space=pltpu.SMEM)


def dot(a, b):
    return lax.dot_general(a, b, (((1,), (0,)), ((), ())), preferred_element_type=f32)


def dot_t(a, b):
    return lax.dot_general(a, b, (((1,), (1,)), ((), ())), preferred_element_type=f32)


def attend_near_kernel(place, q, kv0, kv1, kvx1, held, stats):
    row = lax.broadcasted_iota(jnp.int32, (BLOCK, BLOCK), 0)
    col = lax.broadcasted_iota(jnp.int32, (BLOCK, BLOCK), 1)
    diff = col - row
    shift1 = jnp.where(place[0] >= 1, 0, jnp.int32(4 * BLOCK))
    past = diff + BLOCK > shift1
    visible = jnp.concatenate([past, past, diff <= 0], axis=1)
    tops = jnp.zeros((BLOCK, HEAD_DIM), f32)
    sums = jnp.zeros((BLOCK, HEAD_DIM), f32)
    for h in range(q.shape[1] // HEAD_DIM):
        s = slice(h * HEAD_DIM, (h + 1) * HEAD_DIM)
        keys = jnp.concatenate([kv[:BLOCK, s] for kv in (kv1, kvx1, kv0)], axis=0)
        values = jnp.concatenate([kv[BLOCK:, s] for kv in (kv1, kvx1, kv0)], axis=0)
        scores = dot_t(q[:, s], keys) * (1.0 / math.sqrt(HEAD_DIM))
        scores = jnp.where(visible, scores, masked_score)
        top = jnp.max(scores, axis=1, keepdims=True)
        expo = jnp.exp(scores - top)
        tops = jnp.where(col == h, top, tops)
        sums = jnp.where(col == h, jnp.sum(expo, axis=1, keepdims=True), sums)
        held[:, s] = dot(expo.astype(bf16), values)
    stats[0] = tops
    stats[1] = sums


def attend_far_kernel(place, q, kv2, kvx0, kvx2, held, stats, res, out, home):
    chip = place[0]
    core = place[1]
    row = lax.broadcasted_iota(jnp.int32, (BLOCK, BLOCK), 0)
    col = lax.broadcasted_iota(jnp.int32, (BLOCK, BLOCK), 1)
    diff = col - row
    big = jnp.int32(4 * BLOCK)
    shift2 = jnp.where(chip >= 2, 0, big)
    shiftx = jnp.where((chip >= 2) | (core == 1), 0, big)
    visible = jnp.concatenate([diff > shift2, diff + BLOCK > shiftx], axis=1)
    z_count, core_count = out.shape[0], out.shape[2]
    for h in range(q.shape[1] // HEAD_DIM):
        s = slice(h * HEAD_DIM, (h + 1) * HEAD_DIM)
        kvx = kvx0[:, s] + kvx2[:, s]
        keys = jnp.concatenate([kv2[:BLOCK, s], kvx[:BLOCK]], axis=0)
        values = jnp.concatenate([kv2[BLOCK:, s], kvx[BLOCK:]], axis=0)
        scores = dot_t(q[:, s], keys) * (1.0 / math.sqrt(HEAD_DIM))
        scores = jnp.where(visible, scores, masked_score)
        near_top = stats[0, :, h : h + 1]
        top = jnp.maximum(near_top, jnp.max(scores, axis=1, keepdims=True))
        expo = jnp.exp(scores - top)
        scale = jnp.exp(near_top - top)
        total = stats[1, :, h : h + 1] * scale + jnp.sum(expo, axis=1, keepdims=True)
        summed = held[:, s] * scale + dot(expo.astype(bf16), values)
        stream = res[:, s].astype(f32) + summed * (1.0 / total)
        home[:, s] = stream.astype(bf16)
        out[:, h] = stream.reshape(z_count, core_count, TILE, HEAD_DIM).astype(bf16)


def pick_kernel(index, tiles, out):
    @pl.loop(0, out.shape[0], unroll=8)
    def _(i):
        out[i] = tiles[index[i]]


def project_kernel(tiles, gain, first0, first1, out, held):
    z_count, heads, slots = tiles.shape[:3]
    rows = z_count * slots * TILE
    squares = jnp.zeros((rows, HEAD_DIM), f32)
    for h in range(heads):
        value = tiles[:, h].astype(f32).reshape(rows, HEAD_DIM)
        squares = squares + value * value
        s = slice(h * HEAD_DIM, (h + 1) * HEAD_DIM)
        held[:, s] = (value * gain[:, s]).astype(bf16)
    high = squares.astype(bf16)
    low = (squares - high.astype(f32)).astype(bf16)
    ones = jnp.ones((TILE, HEAD_DIM), bf16)
    total = dot_t(ones, high) + dot_t(ones, low)
    total_high = total.astype(bf16).astype(f32)
    total_rows = jnp.concatenate([total_high, total - total_high], axis=0).astype(bf16)
    x = held[...]
    parts = out.shape[0]
    for t in range(parts):
        width = first0.shape[2]
        out[t, :rows, :width] = dot(x, first0[t]).astype(bf16)
        out[t, :rows, width:] = dot(x, first1[t]).astype(bf16)
        out[t, rows:, :rows] = total_rows
        out[t, rows:, rows:] = total_rows


def hidden_kernel(features, parts, out):
    count = parts.shape[0]
    rows, width = out.shape
    tail = parts.shape[1] - rows
    sums = parts[:, rows:, :rows].reshape(count * tail, rows)
    weight = jnp.full((count * tail, HEAD_DIM), 1.0 / TILE, bf16)
    square = lax.dot_general(
        sums, weight, (((0,), (0,)), ((), ())), preferred_element_type=f32
    )
    factor = lax.rsqrt(square * (1.0 / features) + epsilon)
    half = width // 2
    for k in range(2):
        value = sum(
            parts[t, :rows, k * width : (k + 1) * width].astype(f32) for t in range(count)
        )
        gate = value[:, :half] * factor
        up = value[:, half:] * factor
        out[:, k * half : (k + 1) * half] = (gate / (1.0 + jnp.exp(-gate)) * up).astype(bf16)


def branch_kernel(hidden, down0, down1, out):
    count = hidden.shape[0]
    half = hidden.shape[2] // 2
    first = jnp.concatenate([hidden[t, :, :half] for t in range(count)], axis=1)
    second = jnp.concatenate([hidden[t, :, half:] for t in range(count)], axis=1)
    z_count, heads, slots = out.shape[:3]
    step = 2 * HEAD_DIM
    for s in range(0, heads * HEAD_DIM, step):
        value = dot(first, down0[:, s : s + step]) + dot(second, down1[:, s : s + step])
        for k in range(0, step, HEAD_DIM):
            part = value[:, k : k + HEAD_DIM].reshape(z_count, slots, TILE, HEAD_DIM)
            out[:, (s + k) // HEAD_DIM] = part.astype(bf16)


def finish_kernel(home, branch, out):
    for h in range(branch.shape[1]):
        s = slice(h * HEAD_DIM, (h + 1) * HEAD_DIM)
        value = branch[:, h].astype(f32).reshape(home.shape[0], HEAD_DIM)
        out[:, s] = (home[:, s].astype(f32) + value).astype(bf16)


def local(
    queries, keys, values, residual_in, norm_gain, routing, gate_weight, up_weight, down_weight
):
    seq_count = lax.axis_size("seq")
    tp_count = lax.axis_size("tp")
    seq_place = lax.axis_index("seq")
    tp_place = lax.axis_index("tp")
    chips = seq_count // 2
    rows, width = queries.shape
    heads = width // HEAD_DIM
    z_count = rows // (2 * TILE)
    slots = 4

    onward = [(i, i + 2) for i in range(seq_count - 2)]
    to_odd = [(i, i + 1) for i in range(0, seq_count, 2)]
    to_even = [(i + 1, i) for i in range(0, seq_count, 2)]
    swap = to_odd + to_even
    same_core = [[c + 2 * i for i in range(chips)] for c in (0, 1)]

    def move(x, route):
        return lax.ppermute(x, "seq", route)

    kv0 = jnp.concatenate([keys, values], axis=0)
    kv1 = move(kv0, onward)
    kv2 = move(kv1, onward)
    kvx0 = move(kv0, to_odd)
    kvx1 = move(kv1, swap)
    kvx2 = move(kv2, to_even)

    gate_own, up_own, down0, kvx0 = lax.optimization_barrier(
        (gate_weight[0], up_weight[0], down_weight[0], kvx0)
    )
    both = jnp.concatenate([gate_own, up_own], axis=1).reshape(tp_count, width, -1)
    first0 = lax.all_to_all(both, "tp", 0, 0, tiled=True)
    down1 = move(down0, swap)
    gain = lax.dynamic_slice_in_dim(norm_gain, tp_place * width, width)[None]

    expert = routing[:, 0]
    block_range = jnp.arange(seq_count, dtype=jnp.int32)
    same = expert[None, :] == expert[:, None]
    rank = jnp.sum(same & (block_range[None, :] < block_range[:, None]), axis=1, dtype=jnp.int32)
    slot_of = expert * slots + rank
    slot_range = jnp.arange(chips * slots, dtype=jnp.int32)
    block_of = jnp.sum(
        jnp.where(slot_range[:, None] == slot_of[None, :], block_range[None, :], 0),
        axis=1,
        dtype=jnp.int32,
    )
    place = jnp.stack([seq_place // 2, seq_place % 2]).astype(jnp.int32)

    held, stats = pl.pallas_call(
        attend_near_kernel,
        out_shape=(
            jax.ShapeDtypeStruct((rows, width), f32),
            jax.ShapeDtypeStruct((2, BLOCK, HEAD_DIM), f32),
        ),
        in_specs=[smem()] + [vmem()] * 4,
        out_specs=(vmem(), vmem()),
        compiler_params=params(),
        name="attend_near",
    )(place, queries, kv0, kv1, kvx1)
    place, block_of, slot_of, gain, first0, down1 = lax.optimization_barrier(
        (place, block_of, slot_of, gain, first0, down1)
    )
    stream, home = pl.pallas_call(
        attend_far_kernel,
        out_shape=(
            jax.ShapeDtypeStruct((z_count, heads, 2, TILE, HEAD_DIM), bf16),
            jax.ShapeDtypeStruct((rows, width), bf16),
        ),
        in_specs=[smem()] + [vmem()] * 7,
        out_specs=(vmem(), vmem()),
        compiler_params=params(),
        name="attend_far",
    )(place, queries, kv2, kvx0, kvx2, held, stats, residual_in)

    tiles = lax.all_to_all(
        stream.reshape(seq_count, TILE, HEAD_DIM), "seq", 0, 0, tiled=True
    )

    def pick(index, source):
        return pl.pallas_call(
            pick_kernel,
            out_shape=jax.ShapeDtypeStruct((index.shape[0], TILE, HEAD_DIM), bf16),
            in_specs=[smem(), vmem()],
            out_specs=vmem(),
            compiler_params=params(),
            name="pick",
        )(index, source)

    def same_core_exchange(x):
        x = x.reshape(chips, slots, TILE, HEAD_DIM)
        return lax.all_to_all(x, "seq", 0, 0, tiled=True, axis_index_groups=same_core)

    tiles, first0 = lax.optimization_barrier((tiles, first0))
    first1 = move(first0, swap)
    arrived = same_core_exchange(pick(block_of, tiles))
    arrived = arrived.reshape(z_count, heads, slots, TILE, HEAD_DIM)
    work = z_count * slots * TILE
    hid = first0.shape[2]
    parts = pl.pallas_call(
        project_kernel,
        out_shape=jax.ShapeDtypeStruct((tp_count, work + 2 * TILE, 2 * hid), bf16),
        in_specs=[vmem()] * 4,
        out_specs=vmem(),
        scratch_shapes=[pltpu.VMEM((work, width), bf16)],
        compiler_params=params(),
        name="project",
    )(arrived, gain, first0, first1)
    parts = lax.all_to_all(parts, "tp", 0, 0, tiled=True)

    def run_hidden(parts_ref, out_ref):
        hidden_kernel(width * tp_count, parts_ref, out_ref)

    hidden = pl.pallas_call(
        run_hidden,
        out_shape=jax.ShapeDtypeStruct((work, hid), bf16),
        in_specs=[vmem()],
        out_specs=vmem(),
        compiler_params=params(),
        name="hidden",
    )(parts)
    hidden = lax.all_gather(hidden, "tp")
    branch = pl.pallas_call(
        branch_kernel,
        out_shape=jax.ShapeDtypeStruct((z_count, heads, slots, TILE, HEAD_DIM), bf16),
        in_specs=[vmem()] * 3,
        out_specs=vmem(),
        compiler_params=params(),
        name="branch",
    )(hidden, down0, down1)
    returned = same_core_exchange(branch).reshape(chips * slots, TILE, HEAD_DIM)
    finished = lax.all_to_all(pick(slot_of, returned), "seq", 0, 0, tiled=True)
    return pl.pallas_call(
        finish_kernel,
        out_shape=jax.ShapeDtypeStruct((rows, width), bf16),
        in_specs=[vmem()] * 2,
        out_specs=vmem(),
        compiler_params=params(),
        name="finish",
    )(home, finished.reshape(stream.shape))


def solution(mesh):
    in_specs = (
        P("seq", "tp"),
        P("seq", "tp"),
        P("seq", "tp"),
        P("seq", "tp"),
        P(),
        P(),
        P("seq", None, "tp"),
        P("seq", None, "tp"),
        P("seq", None, "tp"),
    )
    out_specs = P("seq", "tp")
    return jax.shard_map(local, mesh=mesh, in_specs=in_specs, out_specs=out_specs, check_vma=False)
```

```python
import math

import jax
import jax.numpy as jnp
from jax import lax
from jax.experimental import pallas as pl
from jax.experimental.pallas import tpu as pltpu
from jax.sharding import PartitionSpec as P

HEAD_DIM = 128
BLOCK = 128
WINDOW = 512
TILE = 8

epsilon = 1e-05
masked_score = -1e30
f32 = jnp.float32
bf16 = jnp.bfloat16

VMEM_LIMIT = 14 * 1024 * 1024


def params():
    return pltpu.CompilerParams(vmem_limit_bytes=VMEM_LIMIT)


def vmem():
    return pl.BlockSpec(memory_space=pltpu.VMEM)


def smem():
    return pl.BlockSpec(memory_space=pltpu.SMEM)


def anywhere():
    return pl.BlockSpec(memory_space=pl.ANY)


def dot(a, b):
    return lax.dot_general(a, b, (((1,), (0,)), ((), ())), preferred_element_type=f32)


def dot_t(a, b):
    return lax.dot_general(a, b, (((1,), (1,)), ((), ())), preferred_element_type=f32)


def attend_near_kernel(place, q, kv0, kv1, kvx1, _, held, stats):
    row = lax.broadcasted_iota(jnp.int32, (BLOCK, BLOCK), 0)
    col = lax.broadcasted_iota(jnp.int32, (BLOCK, BLOCK), 1)
    diff = col - row
    shift1 = jnp.where(place[0] >= 1, 0, jnp.int32(4 * BLOCK))
    past = diff + BLOCK > shift1
    visible = jnp.concatenate([past, past, diff <= 0], axis=1)
    tops = jnp.zeros((BLOCK, HEAD_DIM), f32)
    sums = jnp.zeros((BLOCK, HEAD_DIM), f32)
    for h in range(q.shape[1] // HEAD_DIM):
        s = slice(h * HEAD_DIM, (h + 1) * HEAD_DIM)
        keys = jnp.concatenate([kv[:BLOCK, s] for kv in (kv1, kvx1, kv0)], axis=0)
        values = jnp.concatenate([kv[BLOCK:, s] for kv in (kv1, kvx1, kv0)], axis=0)
        scores = dot_t(q[:, s], keys) * (1.0 / math.sqrt(HEAD_DIM))
        scores = jnp.where(visible, scores, masked_score)
        top = jnp.max(scores, axis=1, keepdims=True)
        expo = jnp.exp(scores - top)
        tops = jnp.where(col == h, top, tops)
        sums = jnp.where(col == h, jnp.sum(expo, axis=1, keepdims=True), sums)
        held[:, s] = dot(expo.astype(bf16), values)
    stats[0] = tops
    stats[1] = sums


def attend_far_kernel(place, *refs):
    given, (out, home), scratch, sems = refs[:7], refs[7:9], refs[9:16], refs[16]
    copies = [
        pltpu.make_async_copy(source, target, sems.at[i])
        for i, (source, target) in enumerate(zip(given, scratch))
    ]
    for copy in copies:
        copy.start()
    q, kv2, kvx0, kvx2, held, stats, res = scratch
    chip = place[0]
    core = place[1]
    row = lax.broadcasted_iota(jnp.int32, (BLOCK, BLOCK), 0)
    col = lax.broadcasted_iota(jnp.int32, (BLOCK, BLOCK), 1)
    diff = col - row
    big = jnp.int32(4 * BLOCK)
    shift2 = jnp.where(chip >= 2, 0, big)
    shiftx = jnp.where((chip >= 2) | (core == 1), 0, big)
    visible = jnp.concatenate([diff > shift2, diff + BLOCK > shiftx], axis=1)
    for copy in copies:
        copy.wait()
    z_count, core_count = out.shape[0], out.shape[2]
    for h in range(q.shape[1] // HEAD_DIM):
        s = slice(h * HEAD_DIM, (h + 1) * HEAD_DIM)
        kvx = kvx0[:, s] + kvx2[:, s]
        keys = jnp.concatenate([kv2[:BLOCK, s], kvx[:BLOCK]], axis=0)
        values = jnp.concatenate([kv2[BLOCK:, s], kvx[BLOCK:]], axis=0)
        scores = dot_t(q[:, s], keys) * (1.0 / math.sqrt(HEAD_DIM))
        scores = jnp.where(visible, scores, masked_score)
        near_top = stats[0, :, h : h + 1]
        top = jnp.maximum(near_top, jnp.max(scores, axis=1, keepdims=True))
        expo = jnp.exp(scores - top)
        scale = jnp.exp(near_top - top)
        total = stats[1, :, h : h + 1] * scale + jnp.sum(expo, axis=1, keepdims=True)
        summed = held[:, s] * scale + dot(expo.astype(bf16), values)
        stream = res[:, s].astype(f32) + summed * (1.0 / total)
        home[:, s] = stream.astype(bf16)
        out[:, h] = stream.reshape(z_count, core_count, TILE, HEAD_DIM).astype(bf16)


def pick_kernel(index, tiles, out):
    @pl.loop(0, out.shape[0], unroll=8)
    def _(i):
        out[i] = tiles[index[i]]


def project_kernel(tiles, gain, first0, first1, out, held):
    z_count, heads, slots = tiles.shape[:3]
    rows = z_count * slots * TILE
    squares = jnp.zeros((rows, HEAD_DIM), f32)
    for h in range(heads):
        value = tiles[:, h].astype(f32).reshape(rows, HEAD_DIM)
        squares = squares + value * value
        s = slice(h * HEAD_DIM, (h + 1) * HEAD_DIM)
        held[:, s] = (value * gain[:, s]).astype(bf16)
    high = squares.astype(bf16)
    low = (squares - high.astype(f32)).astype(bf16)
    ones = jnp.ones((TILE, HEAD_DIM), bf16)
    total = dot_t(ones, high) + dot_t(ones, low)
    total_high = total.astype(bf16).astype(f32)
    total_rows = jnp.concatenate([total_high, total - total_high], axis=0).astype(bf16)
    x = held[...]
    parts = out.shape[0]
    for t in range(parts):
        width = first0.shape[2]
        out[t, :rows, :width] = dot(x, first0[t]).astype(bf16)
        out[t, :rows, width:] = dot(x, first1[t]).astype(bf16)
        out[t, rows:, :rows] = total_rows
        out[t, rows:, rows:] = total_rows


def hidden_kernel(features, parts, out):
    count = parts.shape[0]
    rows, width = out.shape
    tail = parts.shape[1] - rows
    sums = parts[:, rows:, :rows].reshape(count * tail, rows)
    weight = jnp.full((count * tail, HEAD_DIM), 1.0 / TILE, bf16)
    square = lax.dot_general(
        sums, weight, (((0,), (0,)), ((), ())), preferred_element_type=f32
    )
    factor = lax.rsqrt(square * (1.0 / features) + epsilon)
    half = width // 2
    for k in range(2):
        value = sum(
            parts[t, :rows, k * width : (k + 1) * width].astype(f32) for t in range(count)
        )
        gate = value[:, :half] * factor
        up = value[:, half:] * factor
        out[:, k * half : (k + 1) * half] = (gate / (1.0 + jnp.exp(-gate)) * up).astype(bf16)


def branch_kernel(hidden, down0, down1, out):
    count = hidden.shape[0]
    half = hidden.shape[2] // 2
    first = jnp.concatenate([hidden[t, :, :half] for t in range(count)], axis=1)
    second = jnp.concatenate([hidden[t, :, half:] for t in range(count)], axis=1)
    z_count, heads, slots = out.shape[:3]
    step = 2 * HEAD_DIM
    for s in range(0, heads * HEAD_DIM, step):
        value = dot(first, down0[:, s : s + step]) + dot(second, down1[:, s : s + step])
        for k in range(0, step, HEAD_DIM):
            part = value[:, k : k + HEAD_DIM].reshape(z_count, slots, TILE, HEAD_DIM)
            out[:, (s + k) // HEAD_DIM] = part.astype(bf16)


def finish_kernel(home, branch, out):
    for h in range(branch.shape[1]):
        s = slice(h * HEAD_DIM, (h + 1) * HEAD_DIM)
        value = branch[:, h].astype(f32).reshape(home.shape[0], HEAD_DIM)
        out[:, s] = (home[:, s].astype(f32) + value).astype(bf16)


def local(
    queries, keys, values, residual_in, norm_gain, routing, gate_weight, up_weight, down_weight
):
    seq_count = lax.axis_size("seq")
    tp_count = lax.axis_size("tp")
    seq_place = lax.axis_index("seq")
    tp_place = lax.axis_index("tp")
    chips = seq_count // 2
    rows, width = queries.shape
    heads = width // HEAD_DIM
    z_count = rows // (2 * TILE)
    slots = 4

    onward = [(i, i + 2) for i in range(seq_count - 2)]
    to_odd = [(i, i + 1) for i in range(0, seq_count, 2)]
    to_even = [(i + 1, i) for i in range(0, seq_count, 2)]
    swap = to_odd + to_even
    same_core = [[c + 2 * i for i in range(chips)] for c in (0, 1)]

    def move(x, route):
        return lax.ppermute(x, "seq", route)

    kv0 = jnp.concatenate([keys, values], axis=0)
    kv1 = move(kv0, onward)
    kv2 = move(kv1, onward)
    kvx0 = move(kv0, to_odd)
    kvx1 = move(kv1, swap)
    kvx2 = move(kv2, to_even)

    gate_own, up_own, down0, kv0 = lax.optimization_barrier(
        (gate_weight[0], up_weight[0], down_weight[0], kv0)
    )
    both = jnp.concatenate([gate_own, up_own], axis=1).reshape(tp_count, width, -1)
    first0 = lax.all_to_all(both, "tp", 0, 0, tiled=True)
    down1 = move(down0, swap)
    gain = lax.dynamic_slice_in_dim(norm_gain, tp_place * width, width)[None]

    expert = routing[:, 0]
    block_range = jnp.arange(seq_count, dtype=jnp.int32)
    same = expert[None, :] == expert[:, None]
    rank = jnp.sum(same & (block_range[None, :] < block_range[:, None]), axis=1, dtype=jnp.int32)
    slot_of = expert * slots + rank
    slot_range = jnp.arange(chips * slots, dtype=jnp.int32)
    block_of = jnp.sum(
        jnp.where(slot_range[:, None] == slot_of[None, :], block_range[None, :], 0),
        axis=1,
        dtype=jnp.int32,
    )
    place = jnp.stack([seq_place // 2, seq_place % 2]).astype(jnp.int32)

    place, block_of, slot_of, gain, first0, down1 = lax.optimization_barrier(
        (place, block_of, slot_of, gain, first0, down1)
    )
    held, stats = pl.pallas_call(
        attend_near_kernel,
        out_shape=(
            jax.ShapeDtypeStruct((rows, width), f32),
            jax.ShapeDtypeStruct((2, BLOCK, HEAD_DIM), f32),
        ),
        in_specs=[smem()] + [vmem()] * 5,
        out_specs=(vmem(), vmem()),
        compiler_params=params(),
        name="attend_near",
    )(place, queries, kv0, kv1, kvx1, residual_in)
    pair = pltpu.VMEM((2 * rows, width), bf16)
    single = pltpu.VMEM((rows, width), bf16)
    stream, home = pl.pallas_call(
        attend_far_kernel,
        out_shape=(
            jax.ShapeDtypeStruct((z_count, heads, 2, TILE, HEAD_DIM), bf16),
            jax.ShapeDtypeStruct((rows, width), bf16),
        ),
        in_specs=[smem()] + [anywhere()] * 7,
        out_specs=(vmem(), vmem()),
        scratch_shapes=[
            single,
            pair,
            pair,
            pair,
            pltpu.VMEM((rows, width), f32),
            pltpu.VMEM((2, BLOCK, HEAD_DIM), f32),
            single,
            pltpu.SemaphoreType.DMA((7,)),
        ],
        compiler_params=params(),
        name="attend_far",
    )(place, queries, kv2, kvx0, kvx2, held, stats, residual_in)

    tiles = lax.all_to_all(
        stream.reshape(seq_count, TILE, HEAD_DIM), "seq", 0, 0, tiled=True
    )

    def pick(index, source):
        return pl.pallas_call(
            pick_kernel,
            out_shape=jax.ShapeDtypeStruct((index.shape[0], TILE, HEAD_DIM), bf16),
            in_specs=[smem(), vmem()],
            out_specs=vmem(),
            compiler_params=params(),
            name="pick",
        )(index, source)

    def same_core_exchange(x):
        x = x.reshape(chips, slots, TILE, HEAD_DIM)
        return lax.all_to_all(x, "seq", 0, 0, tiled=True, axis_index_groups=same_core)

    tiles, first0 = lax.optimization_barrier((tiles, first0))
    first1 = move(first0, swap)
    arrived = same_core_exchange(pick(block_of, tiles))
    arrived = arrived.reshape(z_count, heads, slots, TILE, HEAD_DIM)
    work = z_count * slots * TILE
    hid = first0.shape[2]
    parts = pl.pallas_call(
        project_kernel,
        out_shape=jax.ShapeDtypeStruct((tp_count, work + 2 * TILE, 2 * hid), bf16),
        in_specs=[vmem()] * 4,
        out_specs=vmem(),
        scratch_shapes=[pltpu.VMEM((work, width), bf16)],
        compiler_params=params(),
        name="project",
    )(arrived, gain, first0, first1)
    parts = lax.all_to_all(parts, "tp", 0, 0, tiled=True)

    def run_hidden(parts_ref, out_ref):
        hidden_kernel(width * tp_count, parts_ref, out_ref)

    hidden = pl.pallas_call(
        run_hidden,
        out_shape=jax.ShapeDtypeStruct((work, hid), bf16),
        in_specs=[vmem()],
        out_specs=vmem(),
        compiler_params=params(),
        name="hidden",
    )(parts)
    hidden = lax.all_gather(hidden, "tp")
    branch = pl.pallas_call(
        branch_kernel,
        out_shape=jax.ShapeDtypeStruct((z_count, heads, slots, TILE, HEAD_DIM), bf16),
        in_specs=[vmem()] * 3,
        out_specs=vmem(),
        compiler_params=params(),
        name="branch",
    )(hidden, down0, down1)
    returned = same_core_exchange(branch).reshape(chips * slots, TILE, HEAD_DIM)
    finished = lax.all_to_all(pick(slot_of, returned), "seq", 0, 0, tiled=True)
    return pl.pallas_call(
        finish_kernel,
        out_shape=jax.ShapeDtypeStruct((rows, width), bf16),
        in_specs=[vmem()] * 2,
        out_specs=vmem(),
        compiler_params=params(),
        name="finish",
    )(home, finished.reshape(stream.shape))


def solution(mesh):
    in_specs = (
        P("seq", "tp"),
        P("seq", "tp"),
        P("seq", "tp"),
        P("seq", "tp"),
        P(),
        P(),
        P("seq", None, "tp"),
        P("seq", None, "tp"),
        P("seq", None, "tp"),
    )
    out_specs = P("seq", "tp")
    return jax.shard_map(local, mesh=mesh, in_specs=in_specs, out_specs=out_specs, check_vma=False)
```

```python
import math

import jax
import jax.numpy as jnp
from jax import lax
from jax.experimental import pallas as pl
from jax.experimental.pallas import tpu as pltpu
from jax.sharding import PartitionSpec as P

HEAD_DIM = 128
BLOCK = 128
WINDOW = 512
TILE = 8

epsilon = 1e-05
masked_score = -1e30
f32 = jnp.float32
bf16 = jnp.bfloat16

VMEM_LIMIT = 14 * 1024 * 1024


def params():
    return pltpu.CompilerParams(vmem_limit_bytes=VMEM_LIMIT)


def vmem():
    return pl.BlockSpec(memory_space=pltpu.VMEM)


def smem():
    return pl.BlockSpec(memory_space=pltpu.SMEM)


def dot(a, b):
    return lax.dot_general(a, b, (((1,), (0,)), ((), ())), preferred_element_type=f32)


def dot_t(a, b):
    return lax.dot_general(a, b, (((1,), (1,)), ((), ())), preferred_element_type=f32)


def attend_near_kernel(place, q, kv0, kv1, kvx1, _, held, stats):
    row = lax.broadcasted_iota(jnp.int32, (BLOCK, BLOCK), 0)
    col = lax.broadcasted_iota(jnp.int32, (BLOCK, BLOCK), 1)
    diff = col - row
    shift1 = jnp.where(place[0] >= 1, 0, jnp.int32(4 * BLOCK))
    past = diff + BLOCK > shift1
    visible = jnp.concatenate([past, past, diff <= 0], axis=1)
    tops = jnp.zeros((BLOCK, HEAD_DIM), f32)
    sums = jnp.zeros((BLOCK, HEAD_DIM), f32)
    for h in range(q.shape[1] // HEAD_DIM):
        s = slice(h * HEAD_DIM, (h + 1) * HEAD_DIM)
        keys = jnp.concatenate([kv[:BLOCK, s] for kv in (kv1, kvx1, kv0)], axis=0)
        values = jnp.concatenate([kv[BLOCK:, s] for kv in (kv1, kvx1, kv0)], axis=0)
        scores = dot_t(q[:, s], keys) * (1.0 / math.sqrt(HEAD_DIM))
        scores = jnp.where(visible, scores, masked_score)
        top = jnp.max(scores, axis=1, keepdims=True)
        expo = jnp.exp(scores - top)
        tops = jnp.where(col == h, top, tops)
        sums = jnp.where(col == h, jnp.sum(expo, axis=1, keepdims=True), sums)
        held[:, s] = dot(expo.astype(bf16), values)
    stats[0] = tops
    stats[1] = sums


def attend_far_kernel(place, q, kv2, kvx0, kvx2, held, stats, res, out, home):
    chip = place[0]
    core = place[1]
    row = lax.broadcasted_iota(jnp.int32, (BLOCK, BLOCK), 0)
    col = lax.broadcasted_iota(jnp.int32, (BLOCK, BLOCK), 1)
    diff = col - row
    big = jnp.int32(4 * BLOCK)
    shift2 = jnp.where(chip >= 2, 0, big)
    shiftx = jnp.where((chip >= 2) | (core == 1), 0, big)
    visible = jnp.concatenate([diff > shift2, diff + BLOCK > shiftx], axis=1)
    z_count, core_count = out.shape[0], out.shape[2]
    for h in range(q.shape[1] // HEAD_DIM):
        s = slice(h * HEAD_DIM, (h + 1) * HEAD_DIM)
        kvx = kvx0[:, s] + kvx2[:, s]
        keys = jnp.concatenate([kv2[:BLOCK, s], kvx[:BLOCK]], axis=0)
        values = jnp.concatenate([kv2[BLOCK:, s], kvx[BLOCK:]], axis=0)
        scores = dot_t(q[:, s], keys) * (1.0 / math.sqrt(HEAD_DIM))
        scores = jnp.where(visible, scores, masked_score)
        near_top = stats[0, :, h : h + 1]
        top = jnp.maximum(near_top, jnp.max(scores, axis=1, keepdims=True))
        expo = jnp.exp(scores - top)
        scale = jnp.exp(near_top - top)
        total = stats[1, :, h : h + 1] * scale + jnp.sum(expo, axis=1, keepdims=True)
        summed = held[:, s] * scale + dot(expo.astype(bf16), values)
        stream = res[:, s].astype(f32) + summed * (1.0 / total)
        home[:, s] = stream.astype(bf16)
        out[:, h] = stream.reshape(z_count, core_count, TILE, HEAD_DIM).astype(bf16)


def pick_kernel(index, tiles, out):
    @pl.loop(0, out.shape[0], unroll=8)
    def _(i):
        out[i] = tiles[index[i]]


def project_kernel(tiles, gain, first0, first1, out, held):
    z_count, heads, slots = tiles.shape[:3]
    rows = z_count * slots * TILE
    squares = jnp.zeros((rows, HEAD_DIM), f32)
    for h in range(heads):
        value = tiles[:, h].astype(f32).reshape(rows, HEAD_DIM)
        squares = squares + value * value
        s = slice(h * HEAD_DIM, (h + 1) * HEAD_DIM)
        held[:, s] = (value * gain[:, s]).astype(bf16)
    high = squares.astype(bf16)
    low = (squares - high.astype(f32)).astype(bf16)
    ones = jnp.ones((TILE, HEAD_DIM), bf16)
    total = dot_t(ones, high) + dot_t(ones, low)
    total_high = total.astype(bf16).astype(f32)
    total_rows = jnp.concatenate([total_high, total - total_high], axis=0).astype(bf16)
    x = held[...]
    parts = out.shape[0]
    for t in range(parts):
        width = first0.shape[2]
        out[t, :rows, :width] = dot(x, first0[t]).astype(bf16)
        out[t, :rows, width:] = dot(x, first1[t]).astype(bf16)
        out[t, rows:, :rows] = total_rows
        out[t, rows:, rows:] = total_rows


def hidden_kernel(features, parts, out):
    count = parts.shape[0]
    rows, width = out.shape
    tail = parts.shape[1] - rows
    sums = parts[:, rows:, :rows].reshape(count * tail, rows)
    weight = jnp.full((count * tail, HEAD_DIM), 1.0 / TILE, bf16)
    square = lax.dot_general(
        sums, weight, (((0,), (0,)), ((), ())), preferred_element_type=f32
    )
    factor = lax.rsqrt(square * (1.0 / features) + epsilon)
    half = width // 2
    for k in range(2):
        value = sum(
            parts[t, :rows, k * width : (k + 1) * width].astype(f32) for t in range(count)
        )
        gate = value[:, :half] * factor
        up = value[:, half:] * factor
        out[:, k * half : (k + 1) * half] = (gate / (1.0 + jnp.exp(-gate)) * up).astype(bf16)


def branch_kernel(hidden, down0, down1, out):
    count = hidden.shape[0]
    half = hidden.shape[2] // 2
    first = jnp.concatenate([hidden[t, :, :half] for t in range(count)], axis=1)
    second = jnp.concatenate([hidden[t, :, half:] for t in range(count)], axis=1)
    z_count, heads, slots = out.shape[:3]
    step = 2 * HEAD_DIM
    for s in range(0, heads * HEAD_DIM, step):
        value = dot(first, down0[:, s : s + step]) + dot(second, down1[:, s : s + step])
        for k in range(0, step, HEAD_DIM):
            part = value[:, k : k + HEAD_DIM].reshape(z_count, slots, TILE, HEAD_DIM)
            out[:, (s + k) // HEAD_DIM] = part.astype(bf16)


def finish_kernel(home, branch, out):
    for h in range(branch.shape[1]):
        s = slice(h * HEAD_DIM, (h + 1) * HEAD_DIM)
        value = branch[:, h].astype(f32).reshape(home.shape[0], HEAD_DIM)
        out[:, s] = (home[:, s].astype(f32) + value).astype(bf16)


def local(
    queries, keys, values, residual_in, norm_gain, routing, gate_weight, up_weight, down_weight
):
    seq_count = lax.axis_size("seq")
    tp_count = lax.axis_size("tp")
    seq_place = lax.axis_index("seq")
    tp_place = lax.axis_index("tp")
    chips = seq_count // 2
    rows, width = queries.shape
    heads = width // HEAD_DIM
    z_count = rows // (2 * TILE)
    slots = 4

    onward = [(i, i + 2) for i in range(seq_count - 2)]
    to_odd = [(i, i + 1) for i in range(0, seq_count, 2)]
    to_even = [(i + 1, i) for i in range(0, seq_count, 2)]
    swap = to_odd + to_even
    same_core = [[c + 2 * i for i in range(chips)] for c in (0, 1)]

    def move(x, route):
        return lax.ppermute(x, "seq", route)

    kv0 = jnp.concatenate([keys, values], axis=0)
    kv1 = move(kv0, onward)
    kv2 = move(kv1, onward)
    kvx0 = move(kv0, to_odd)
    kvx1 = move(kv1, swap)

    gate_own, up_own, down0, kv0 = lax.optimization_barrier(
        (gate_weight[0], up_weight[0], down_weight[0], kv0)
    )
    both = jnp.concatenate([gate_own, up_own], axis=1).reshape(tp_count, width, -1)
    first0 = lax.all_to_all(both, "tp", 0, 0, tiled=True)
    down1 = move(down0, swap)
    gain = lax.dynamic_slice_in_dim(norm_gain, tp_place * width, width)[None]

    expert = routing[:, 0]
    block_range = jnp.arange(seq_count, dtype=jnp.int32)
    same = expert[None, :] == expert[:, None]
    rank = jnp.sum(same & (block_range[None, :] < block_range[:, None]), axis=1, dtype=jnp.int32)
    slot_of = expert * slots + rank
    slot_range = jnp.arange(chips * slots, dtype=jnp.int32)
    block_of = jnp.sum(
        jnp.where(slot_range[:, None] == slot_of[None, :], block_range[None, :], 0),
        axis=1,
        dtype=jnp.int32,
    )
    place = jnp.stack([seq_place // 2, seq_place % 2]).astype(jnp.int32)

    place, block_of, slot_of, gain = lax.optimization_barrier((place, block_of, slot_of, gain))
    held, stats = pl.pallas_call(
        attend_near_kernel,
        out_shape=(
            jax.ShapeDtypeStruct((rows, width), f32),
            jax.ShapeDtypeStruct((2, BLOCK, HEAD_DIM), f32),
        ),
        in_specs=[smem()] + [vmem()] * 5,
        out_specs=(vmem(), vmem()),
        compiler_params=params(),
        name="attend_near",
    )(place, queries, kv0, kv1, kvx1, residual_in)
    kv2, held, stats = lax.optimization_barrier((kv2, held, stats))
    kvx2 = move(kv2, to_even)
    stream, home = pl.pallas_call(
        attend_far_kernel,
        out_shape=(
            jax.ShapeDtypeStruct((z_count, heads, 2, TILE, HEAD_DIM), bf16),
            jax.ShapeDtypeStruct((rows, width), bf16),
        ),
        in_specs=[smem()] + [vmem()] * 7,
        out_specs=(vmem(), vmem()),
        compiler_params=params(),
        name="attend_far",
    )(place, queries, kv2, kvx0, kvx2, held, stats, residual_in)
    stream, first0, down1 = lax.optimization_barrier((stream, first0, down1))

    tiles = lax.all_to_all(
        stream.reshape(seq_count, TILE, HEAD_DIM), "seq", 0, 0, tiled=True
    )

    def pick(index, source):
        return pl.pallas_call(
            pick_kernel,
            out_shape=jax.ShapeDtypeStruct((index.shape[0], TILE, HEAD_DIM), bf16),
            in_specs=[smem(), vmem()],
            out_specs=vmem(),
            compiler_params=params(),
            name="pick",
        )(index, source)

    def same_core_exchange(x):
        x = x.reshape(chips, slots, TILE, HEAD_DIM)
        return lax.all_to_all(x, "seq", 0, 0, tiled=True, axis_index_groups=same_core)

    tiles, first0 = lax.optimization_barrier((tiles, first0))
    first1 = move(first0, swap)
    arrived = same_core_exchange(pick(block_of, tiles))
    arrived = arrived.reshape(z_count, heads, slots, TILE, HEAD_DIM)
    work = z_count * slots * TILE
    hid = first0.shape[2]
    parts = pl.pallas_call(
        project_kernel,
        out_shape=jax.ShapeDtypeStruct((tp_count, work + 2 * TILE, 2 * hid), bf16),
        in_specs=[vmem()] * 4,
        out_specs=vmem(),
        scratch_shapes=[pltpu.VMEM((work, width), bf16)],
        compiler_params=params(),
        name="project",
    )(arrived, gain, first0, first1)
    parts = lax.all_to_all(parts, "tp", 0, 0, tiled=True)

    def run_hidden(parts_ref, out_ref):
        hidden_kernel(width * tp_count, parts_ref, out_ref)

    hidden = pl.pallas_call(
        run_hidden,
        out_shape=jax.ShapeDtypeStruct((work, hid), bf16),
        in_specs=[vmem()],
        out_specs=vmem(),
        compiler_params=params(),
        name="hidden",
    )(parts)
    hidden = lax.all_gather(hidden, "tp")
    branch = pl.pallas_call(
        branch_kernel,
        out_shape=jax.ShapeDtypeStruct((z_count, heads, slots, TILE, HEAD_DIM), bf16),
        in_specs=[vmem()] * 3,
        out_specs=vmem(),
        compiler_params=params(),
        name="branch",
    )(hidden, down0, down1)
    returned = same_core_exchange(branch).reshape(chips * slots, TILE, HEAD_DIM)
    finished = lax.all_to_all(pick(slot_of, returned), "seq", 0, 0, tiled=True)
    return pl.pallas_call(
        finish_kernel,
        out_shape=jax.ShapeDtypeStruct((rows, width), bf16),
        in_specs=[vmem()] * 2,
        out_specs=vmem(),
        compiler_params=params(),
        name="finish",
    )(home, finished.reshape(stream.shape))


def solution(mesh):
    in_specs = (
        P("seq", "tp"),
        P("seq", "tp"),
        P("seq", "tp"),
        P("seq", "tp"),
        P(),
        P(),
        P("seq", None, "tp"),
        P("seq", None, "tp"),
        P("seq", None, "tp"),
    )
    out_specs = P("seq", "tp")
    return jax.shard_map(local, mesh=mesh, in_specs=in_specs, out_specs=out_specs, check_vma=False)
```

```python
import math

import jax
import jax.numpy as jnp
from jax import lax
from jax.experimental import pallas as pl
from jax.experimental.pallas import tpu as pltpu
from jax.sharding import PartitionSpec as P

HEAD_DIM = 128
BLOCK = 128
WINDOW = 512
TILE = 8

epsilon = 1e-05
masked_score = -1e30
f32 = jnp.float32
bf16 = jnp.bfloat16

VMEM_LIMIT = 14 * 1024 * 1024


def params():
    return pltpu.CompilerParams(vmem_limit_bytes=VMEM_LIMIT)


def vmem():
    return pl.BlockSpec(memory_space=pltpu.VMEM)


def smem():
    return pl.BlockSpec(memory_space=pltpu.SMEM)


def dot(a, b):
    return lax.dot_general(a, b, (((1,), (0,)), ((), ())), preferred_element_type=f32)


def dot_t(a, b):
    return lax.dot_general(a, b, (((1,), (1,)), ((), ())), preferred_element_type=f32)


def attend_near_kernel(place, q, k0, k1, kx1, v0, v1, vx1, _, held, stats):
    row = lax.broadcasted_iota(jnp.int32, (BLOCK, BLOCK), 0)
    col = lax.broadcasted_iota(jnp.int32, (BLOCK, BLOCK), 1)
    diff = col - row
    shift1 = jnp.where(place[0] >= 1, 0, jnp.int32(4 * BLOCK))
    past = diff + BLOCK > shift1
    visible = jnp.concatenate([past, past, diff <= 0], axis=1)
    tops = jnp.zeros((BLOCK, HEAD_DIM), f32)
    sums = jnp.zeros((BLOCK, HEAD_DIM), f32)
    for h in range(q.shape[1] // HEAD_DIM):
        s = slice(h * HEAD_DIM, (h + 1) * HEAD_DIM)
        keys = jnp.concatenate([k1[:, s], kx1[:, s], k0[:, s]], axis=0)
        values = jnp.concatenate([v1[:, s], vx1[:, s], v0[:, s]], axis=0)
        scores = dot_t(q[:, s], keys) * (1.0 / math.sqrt(HEAD_DIM))
        scores = jnp.where(visible, scores, masked_score)
        top = jnp.max(scores, axis=1, keepdims=True)
        expo = jnp.exp(scores - top)
        tops = jnp.where(col == h, top, tops)
        sums = jnp.where(col == h, jnp.sum(expo, axis=1, keepdims=True), sums)
        held[:, s] = dot(expo.astype(bf16), values)
    stats[0] = tops
    stats[1] = sums


def attend_far_kernel(place, q, k2, kx0, kx2, v2, vx0, vx2, held, stats, res, out, home):
    chip = place[0]
    core = place[1]
    row = lax.broadcasted_iota(jnp.int32, (BLOCK, BLOCK), 0)
    col = lax.broadcasted_iota(jnp.int32, (BLOCK, BLOCK), 1)
    diff = col - row
    big = jnp.int32(4 * BLOCK)
    shift2 = jnp.where(chip >= 2, 0, big)
    shiftx = jnp.where((chip >= 2) | (core == 1), 0, big)
    visible = jnp.concatenate([diff > shift2, diff + BLOCK > shiftx], axis=1)
    z_count, core_count = out.shape[0], out.shape[2]
    for h in range(q.shape[1] // HEAD_DIM):
        s = slice(h * HEAD_DIM, (h + 1) * HEAD_DIM)
        keys = jnp.concatenate([k2[:, s], kx0[:, s] + kx2[:, s]], axis=0)
        values = jnp.concatenate([v2[:, s], vx0[:, s] + vx2[:, s]], axis=0)
        scores = dot_t(q[:, s], keys) * (1.0 / math.sqrt(HEAD_DIM))
        scores = jnp.where(visible, scores, masked_score)
        near_top = stats[0, :, h : h + 1]
        top = jnp.maximum(near_top, jnp.max(scores, axis=1, keepdims=True))
        expo = jnp.exp(scores - top)
        scale = jnp.exp(near_top - top)
        total = stats[1, :, h : h + 1] * scale + jnp.sum(expo, axis=1, keepdims=True)
        summed = held[:, s] * scale + dot(expo.astype(bf16), values)
        stream = res[:, s].astype(f32) + summed * (1.0 / total)
        home[:, s] = stream.astype(bf16)
        out[:, h] = stream.reshape(z_count, core_count, TILE, HEAD_DIM).astype(bf16)


def pick_kernel(index, tiles, out):
    @pl.loop(0, out.shape[0], unroll=8)
    def _(i):
        out[i] = tiles[index[i]]


def project_kernel(tiles, gain, first0, first1, out, held):
    z_count, heads, slots = tiles.shape[:3]
    rows = z_count * slots * TILE
    squares = jnp.zeros((rows, HEAD_DIM), f32)
    for h in range(heads):
        value = tiles[:, h].astype(f32).reshape(rows, HEAD_DIM)
        squares = squares + value * value
        s = slice(h * HEAD_DIM, (h + 1) * HEAD_DIM)
        held[:, s] = (value * gain[:, s]).astype(bf16)
    high = squares.astype(bf16)
    low = (squares - high.astype(f32)).astype(bf16)
    ones = jnp.ones((TILE, HEAD_DIM), bf16)
    total = dot_t(ones, high) + dot_t(ones, low)
    total_high = total.astype(bf16).astype(f32)
    total_rows = jnp.concatenate([total_high, total - total_high], axis=0).astype(bf16)
    x = held[...]
    parts = out.shape[0]
    for t in range(parts):
        width = first0.shape[2]
        out[t, :rows, :width] = dot(x, first0[t]).astype(bf16)
        out[t, :rows, width:] = dot(x, first1[t]).astype(bf16)
        out[t, rows:, :rows] = total_rows
        out[t, rows:, rows:] = total_rows


def hidden_kernel(features, parts, out):
    count = parts.shape[0]
    rows, width = out.shape
    tail = parts.shape[1] - rows
    sums = parts[:, rows:, :rows].reshape(count * tail, rows)
    weight = jnp.full((count * tail, HEAD_DIM), 1.0 / TILE, bf16)
    square = lax.dot_general(
        sums, weight, (((0,), (0,)), ((), ())), preferred_element_type=f32
    )
    factor = lax.rsqrt(square * (1.0 / features) + epsilon)
    half = width // 2
    for k in range(2):
        value = sum(
            parts[t, :rows, k * width : (k + 1) * width].astype(f32) for t in range(count)
        )
        gate = value[:, :half] * factor
        up = value[:, half:] * factor
        out[:, k * half : (k + 1) * half] = (gate / (1.0 + jnp.exp(-gate)) * up).astype(bf16)


def branch_kernel(hidden, down0, down1, out):
    count = hidden.shape[0]
    half = hidden.shape[2] // 2
    first = jnp.concatenate([hidden[t, :, :half] for t in range(count)], axis=1)
    second = jnp.concatenate([hidden[t, :, half:] for t in range(count)], axis=1)
    z_count, heads, slots = out.shape[:3]
    step = 2 * HEAD_DIM
    for s in range(0, heads * HEAD_DIM, step):
        value = dot(first, down0[:, s : s + step]) + dot(second, down1[:, s : s + step])
        for k in range(0, step, HEAD_DIM):
            part = value[:, k : k + HEAD_DIM].reshape(z_count, slots, TILE, HEAD_DIM)
            out[:, (s + k) // HEAD_DIM] = part.astype(bf16)


def finish_kernel(home, branch, out):
    for h in range(branch.shape[1]):
        s = slice(h * HEAD_DIM, (h + 1) * HEAD_DIM)
        value = branch[:, h].astype(f32).reshape(home.shape[0], HEAD_DIM)
        out[:, s] = (home[:, s].astype(f32) + value).astype(bf16)


def local(
    queries, keys, values, residual_in, norm_gain, routing, gate_weight, up_weight, down_weight
):
    seq_count = lax.axis_size("seq")
    tp_count = lax.axis_size("tp")
    seq_place = lax.axis_index("seq")
    tp_place = lax.axis_index("tp")
    chips = seq_count // 2
    rows, width = queries.shape
    heads = width // HEAD_DIM
    z_count = rows // (2 * TILE)
    slots = 4

    onward = [(i, i + 2) for i in range(seq_count - 2)]
    to_odd = [(i, i + 1) for i in range(0, seq_count, 2)]
    to_even = [(i + 1, i) for i in range(0, seq_count, 2)]
    swap = to_odd + to_even
    same_core = [[c + 2 * i for i in range(chips)] for c in (0, 1)]

    def move(x, route):
        return lax.ppermute(x, "seq", route)

    k1 = move(keys, onward)
    v1 = move(values, onward)
    k2 = move(k1, onward)
    v2 = move(v1, onward)
    kx0 = move(keys, to_odd)
    vx0 = move(values, to_odd)
    kx1 = move(k1, swap)
    vx1 = move(v1, swap)

    gate_own, up_own, down0 = gate_weight[0], up_weight[0], down_weight[0]
    def by_features_now(w):
        return lax.all_to_all(w.reshape(tp_count, width, -1), "tp", 0, 0, tiled=True)

    def by_features(w):
        w = lax.all_gather(w, "tp")
        return lax.dynamic_slice_in_dim(w, tp_place * width, width, 1)

    up0 = by_features_now(up_own)
    gate0 = by_features(gate_own)
    down1 = move(down0, swap)
    gain = lax.dynamic_slice_in_dim(norm_gain, tp_place * width, width)[None]

    expert = routing[:, 0]
    block_range = jnp.arange(seq_count, dtype=jnp.int32)
    same = expert[None, :] == expert[:, None]
    rank = jnp.sum(same & (block_range[None, :] < block_range[:, None]), axis=1, dtype=jnp.int32)
    slot_of = expert * slots + rank
    slot_range = jnp.arange(chips * slots, dtype=jnp.int32)
    block_of = jnp.sum(
        jnp.where(slot_range[:, None] == slot_of[None, :], block_range[None, :], 0),
        axis=1,
        dtype=jnp.int32,
    )
    place = jnp.stack([seq_place // 2, seq_place % 2]).astype(jnp.int32)

    place, block_of, slot_of, gain = lax.optimization_barrier((place, block_of, slot_of, gain))
    held, stats = pl.pallas_call(
        attend_near_kernel,
        out_shape=(
            jax.ShapeDtypeStruct((rows, width), f32),
            jax.ShapeDtypeStruct((2, BLOCK, HEAD_DIM), f32),
        ),
        in_specs=[smem()] + [vmem()] * 8,
        out_specs=(vmem(), vmem()),
        compiler_params=params(),
        name="attend_near",
    )(place, queries, keys, k1, kx1, values, v1, vx1, residual_in)
    k2, v2, held, stats = lax.optimization_barrier((k2, v2, held, stats))
    kx2 = move(k2, to_even)
    vx2 = move(v2, to_even)
    stream, home = pl.pallas_call(
        attend_far_kernel,
        out_shape=(
            jax.ShapeDtypeStruct((z_count, heads, 2, TILE, HEAD_DIM), bf16),
            jax.ShapeDtypeStruct((rows, width), bf16),
        ),
        in_specs=[smem()] + [vmem()] * 10,
        out_specs=(vmem(), vmem()),
        compiler_params=params(),
        name="attend_far",
    )(place, queries, k2, kx0, kx2, v2, vx0, vx2, held, stats, residual_in)

    stream, up0 = lax.optimization_barrier((stream, up0))
    first0 = jnp.concatenate([gate0, up0], axis=2)
    tiles = lax.all_to_all(
        stream.reshape(seq_count, TILE, HEAD_DIM), "seq", 0, 0, tiled=True
    )

    def pick(index, source):
        return pl.pallas_call(
            pick_kernel,
            out_shape=jax.ShapeDtypeStruct((index.shape[0], TILE, HEAD_DIM), bf16),
            in_specs=[smem(), vmem()],
            out_specs=vmem(),
            compiler_params=params(),
            name="pick",
        )(index, source)

    def same_core_exchange(x):
        x = x.reshape(chips, slots, TILE, HEAD_DIM)
        return lax.all_to_all(x, "seq", 0, 0, tiled=True, axis_index_groups=same_core)

    tiles, first0 = lax.optimization_barrier((tiles, first0))
    first1 = move(first0, swap)
    arrived = same_core_exchange(pick(block_of, tiles))
    arrived = arrived.reshape(z_count, heads, slots, TILE, HEAD_DIM)
    work = z_count * slots * TILE
    hid = first0.shape[2]
    parts = pl.pallas_call(
        project_kernel,
        out_shape=jax.ShapeDtypeStruct((tp_count, work + 2 * TILE, 2 * hid), bf16),
        in_specs=[vmem()] * 4,
        out_specs=vmem(),
        scratch_shapes=[pltpu.VMEM((work, width), bf16)],
        compiler_params=params(),
        name="project",
    )(arrived, gain, first0, first1)
    parts = lax.all_to_all(parts, "tp", 0, 0, tiled=True)

    def run_hidden(parts_ref, out_ref):
        hidden_kernel(width * tp_count, parts_ref, out_ref)

    hidden = pl.pallas_call(
        run_hidden,
        out_shape=jax.ShapeDtypeStruct((work, hid), bf16),
        in_specs=[vmem()],
        out_specs=vmem(),
        compiler_params=params(),
        name="hidden",
    )(parts)
    hidden = lax.all_gather(hidden, "tp")
    branch = pl.pallas_call(
        branch_kernel,
        out_shape=jax.ShapeDtypeStruct((z_count, heads, slots, TILE, HEAD_DIM), bf16),
        in_specs=[vmem()] * 3,
        out_specs=vmem(),
        compiler_params=params(),
        name="branch",
    )(hidden, down0, down1)
    returned = same_core_exchange(branch).reshape(chips * slots, TILE, HEAD_DIM)
    finished = lax.all_to_all(pick(slot_of, returned), "seq", 0, 0, tiled=True)
    return pl.pallas_call(
        finish_kernel,
        out_shape=jax.ShapeDtypeStruct((rows, width), bf16),
        in_specs=[vmem()] * 2,
        out_specs=vmem(),
        compiler_params=params(),
        name="finish",
    )(home, finished.reshape(stream.shape))


def solution(mesh):
    in_specs = (
        P("seq", "tp"),
        P("seq", "tp"),
        P("seq", "tp"),
        P("seq", "tp"),
        P(),
        P(),
        P("seq", None, "tp"),
        P("seq", None, "tp"),
        P("seq", None, "tp"),
    )
    out_specs = P("seq", "tp")
    return jax.shard_map(local, mesh=mesh, in_specs=in_specs, out_specs=out_specs, check_vma=False)
```

```python
import math

import jax
import jax.numpy as jnp
from jax import lax
from jax.experimental import pallas as pl
from jax.experimental.pallas import tpu as pltpu
from jax.sharding import PartitionSpec as P

HEAD_DIM = 128
BLOCK = 128
WINDOW = 512
TILE = 8

epsilon = 1e-05
masked_score = -1e30
f32 = jnp.float32
bf16 = jnp.bfloat16

VMEM_LIMIT = 14 * 1024 * 1024


def params():
    return pltpu.CompilerParams(vmem_limit_bytes=VMEM_LIMIT)


def vmem():
    return pl.BlockSpec(memory_space=pltpu.VMEM)


def smem():
    return pl.BlockSpec(memory_space=pltpu.SMEM)


def dot(a, b):
    return lax.dot_general(a, b, (((1,), (0,)), ((), ())), preferred_element_type=f32)


def dot_t(a, b):
    return lax.dot_general(a, b, (((1,), (1,)), ((), ())), preferred_element_type=f32)


def attend_near_kernel(place, q, k0, k1, kx1, v0, v1, vx1, _, held, stats):
    row = lax.broadcasted_iota(jnp.int32, (BLOCK, BLOCK), 0)
    col = lax.broadcasted_iota(jnp.int32, (BLOCK, BLOCK), 1)
    diff = col - row
    shift1 = jnp.where(place[0] >= 1, 0, jnp.int32(4 * BLOCK))
    past = diff + BLOCK > shift1
    visible = jnp.concatenate([past, past, diff <= 0], axis=1)
    tops = jnp.zeros((BLOCK, HEAD_DIM), f32)
    sums = jnp.zeros((BLOCK, HEAD_DIM), f32)
    for h in range(q.shape[1] // HEAD_DIM):
        s = slice(h * HEAD_DIM, (h + 1) * HEAD_DIM)
        keys = jnp.concatenate([k1[:, s], kx1[:, s], k0[:, s]], axis=0)
        values = jnp.concatenate([v1[:, s], vx1[:, s], v0[:, s]], axis=0)
        scores = dot_t(q[:, s], keys) * (1.0 / math.sqrt(HEAD_DIM))
        scores = jnp.where(visible, scores, masked_score)
        top = jnp.max(scores, axis=1, keepdims=True)
        expo = jnp.exp(scores - top)
        tops = jnp.where(col == h, top, tops)
        sums = jnp.where(col == h, jnp.sum(expo, axis=1, keepdims=True), sums)
        held[:, s] = dot(expo.astype(bf16), values)
    stats[0] = tops
    stats[1] = sums


def attend_far_kernel(place, q, k2, kx0, kx2, v2, vx0, vx2, held, stats, res, out, home):
    chip = place[0]
    core = place[1]
    row = lax.broadcasted_iota(jnp.int32, (BLOCK, BLOCK), 0)
    col = lax.broadcasted_iota(jnp.int32, (BLOCK, BLOCK), 1)
    diff = col - row
    big = jnp.int32(4 * BLOCK)
    shift2 = jnp.where(chip >= 2, 0, big)
    shiftx = jnp.where((chip >= 2) | (core == 1), 0, big)
    visible = jnp.concatenate([diff > shift2, diff + BLOCK > shiftx], axis=1)
    z_count, core_count = out.shape[0], out.shape[2]
    for h in range(q.shape[1] // HEAD_DIM):
        s = slice(h * HEAD_DIM, (h + 1) * HEAD_DIM)
        keys = jnp.concatenate([k2[:, s], kx0[:, s] + kx2[:, s]], axis=0)
        values = jnp.concatenate([v2[:, s], vx0[:, s] + vx2[:, s]], axis=0)
        scores = dot_t(q[:, s], keys) * (1.0 / math.sqrt(HEAD_DIM))
        scores = jnp.where(visible, scores, masked_score)
        near_top = stats[0, :, h : h + 1]
        top = jnp.maximum(near_top, jnp.max(scores, axis=1, keepdims=True))
        expo = jnp.exp(scores - top)
        scale = jnp.exp(near_top - top)
        total = stats[1, :, h : h + 1] * scale + jnp.sum(expo, axis=1, keepdims=True)
        summed = held[:, s] * scale + dot(expo.astype(bf16), values)
        stream = res[:, s].astype(f32) + summed * (1.0 / total)
        home[:, s] = stream.astype(bf16)
        out[:, h] = stream.reshape(z_count, core_count, TILE, HEAD_DIM).astype(bf16)


def pick_kernel(index, tiles, out):
    @pl.loop(0, out.shape[0], unroll=8)
    def _(i):
        out[i] = tiles[index[i]]


def scale_kernel(tiles, gain, out):
    z_count, heads, slots = tiles.shape[:3]
    rows = z_count * slots * TILE
    count = out.shape[0]
    squares = jnp.zeros((rows, HEAD_DIM), f32)
    for h in range(heads):
        value = tiles[:, h].astype(f32).reshape(rows, HEAD_DIM)
        squares = squares + value * value
        s = slice(h * HEAD_DIM, (h + 1) * HEAD_DIM)
        scaled = (value * gain[:, s]).astype(bf16)
        for t in range(count):
            out[t, :rows, s] = scaled
    high = squares.astype(bf16)
    low = (squares - high.astype(f32)).astype(bf16)
    ones = jnp.ones((TILE, HEAD_DIM), bf16)
    total = dot_t(ones, high) + dot_t(ones, low)
    total_high = total.astype(bf16).astype(f32)
    total_rows = jnp.concatenate([total_high, total - total_high], axis=0).astype(bf16)
    for t in range(count):
        for s in range(0, out.shape[2], rows):
            out[t, rows:, s : s + rows] = total_rows


def hidden_kernel(features, scaled, gate0, gate1, up0, up1, out):
    count = scaled.shape[0]
    rows, width = out.shape
    tail = scaled.shape[1] - rows
    depth = scaled.shape[2]
    sums = scaled[:, rows:, :rows].reshape(count * tail, rows)
    weight = jnp.full((count * tail, HEAD_DIM), 1.0 / TILE, bf16)
    square = lax.dot_general(
        sums, weight, (((0,), (0,)), ((), ())), preferred_element_type=f32
    )
    factor = lax.rsqrt(square * (1.0 / features) + epsilon)
    gate = jnp.zeros((rows, width), f32)
    up = jnp.zeros((rows, width), f32)
    for t in range(count):
        k = slice(t * depth, (t + 1) * depth)
        x = scaled[t, :rows]
        gate = gate + dot(x, jnp.concatenate([gate0[k], gate1[k]], axis=1))
        up = up + dot(x, jnp.concatenate([up0[k], up1[k]], axis=1))
    half = width // 2
    for s in (slice(0, half), slice(half, width)):
        g = gate[:, s] * factor
        out[:, s] = (g / (1.0 + jnp.exp(-g)) * (up[:, s] * factor)).astype(bf16)


def branch_kernel(hidden, down0, down1, out):
    count = hidden.shape[0]
    half = hidden.shape[2] // 2
    first = jnp.concatenate([hidden[t, :, :half] for t in range(count)], axis=1)
    second = jnp.concatenate([hidden[t, :, half:] for t in range(count)], axis=1)
    z_count, heads, slots = out.shape[:3]
    step = 2 * HEAD_DIM
    for s in range(0, heads * HEAD_DIM, step):
        value = dot(first, down0[:, s : s + step]) + dot(second, down1[:, s : s + step])
        for k in range(0, step, HEAD_DIM):
            part = value[:, k : k + HEAD_DIM].reshape(z_count, slots, TILE, HEAD_DIM)
            out[:, (s + k) // HEAD_DIM] = part.astype(bf16)


def finish_kernel(home, branch, out):
    for h in range(branch.shape[1]):
        s = slice(h * HEAD_DIM, (h + 1) * HEAD_DIM)
        value = branch[:, h].astype(f32).reshape(home.shape[0], HEAD_DIM)
        out[:, s] = (home[:, s].astype(f32) + value).astype(bf16)


def local(
    queries, keys, values, residual_in, norm_gain, routing, gate_weight, up_weight, down_weight
):
    seq_count = lax.axis_size("seq")
    tp_count = lax.axis_size("tp")
    seq_place = lax.axis_index("seq")
    tp_place = lax.axis_index("tp")
    chips = seq_count // 2
    rows, width = queries.shape
    heads = width // HEAD_DIM
    z_count = rows // (2 * TILE)
    slots = 4

    onward = [(i, i + 2) for i in range(seq_count - 2)]
    to_odd = [(i, i + 1) for i in range(0, seq_count, 2)]
    to_even = [(i + 1, i) for i in range(0, seq_count, 2)]
    swap = to_odd + to_even
    same_core = [[c + 2 * i for i in range(chips)] for c in (0, 1)]

    def move(x, route):
        return lax.ppermute(x, "seq", route)

    k1 = move(keys, onward)
    v1 = move(values, onward)
    k2 = move(k1, onward)
    v2 = move(v1, onward)
    kx0 = move(keys, to_odd)
    vx0 = move(values, to_odd)
    kx1 = move(k1, swap)
    vx1 = move(v1, swap)

    gate0, up0, down0 = gate_weight[0], up_weight[0], down_weight[0]
    gate1 = move(gate0, swap)
    up1 = move(up0, swap)
    down1 = move(down0, swap)
    gain = lax.dynamic_slice_in_dim(norm_gain, tp_place * width, width)[None]

    expert = routing[:, 0]
    block_range = jnp.arange(seq_count, dtype=jnp.int32)
    same = expert[None, :] == expert[:, None]
    rank = jnp.sum(same & (block_range[None, :] < block_range[:, None]), axis=1, dtype=jnp.int32)
    slot_of = expert * slots + rank
    slot_range = jnp.arange(chips * slots, dtype=jnp.int32)
    block_of = jnp.sum(
        jnp.where(slot_range[:, None] == slot_of[None, :], block_range[None, :], 0),
        axis=1,
        dtype=jnp.int32,
    )
    place = jnp.stack([seq_place // 2, seq_place % 2]).astype(jnp.int32)

    place, block_of, slot_of, gain = lax.optimization_barrier((place, block_of, slot_of, gain))
    held, stats = pl.pallas_call(
        attend_near_kernel,
        out_shape=(
            jax.ShapeDtypeStruct((rows, width), f32),
            jax.ShapeDtypeStruct((2, BLOCK, HEAD_DIM), f32),
        ),
        in_specs=[smem()] + [vmem()] * 8,
        out_specs=(vmem(), vmem()),
        compiler_params=params(),
        name="attend_near",
    )(place, queries, keys, k1, kx1, values, v1, vx1, residual_in)
    k2, v2, held, stats = lax.optimization_barrier((k2, v2, held, stats))
    kx2 = move(k2, to_even)
    vx2 = move(v2, to_even)
    stream, home = pl.pallas_call(
        attend_far_kernel,
        out_shape=(
            jax.ShapeDtypeStruct((z_count, heads, 2, TILE, HEAD_DIM), bf16),
            jax.ShapeDtypeStruct((rows, width), bf16),
        ),
        in_specs=[smem()] + [vmem()] * 10,
        out_specs=(vmem(), vmem()),
        compiler_params=params(),
        name="attend_far",
    )(place, queries, k2, kx0, kx2, v2, vx0, vx2, held, stats, residual_in)

    tiles = lax.all_to_all(
        stream.reshape(seq_count, TILE, HEAD_DIM), "seq", 0, 0, tiled=True
    )

    def pick(index, source):
        return pl.pallas_call(
            pick_kernel,
            out_shape=jax.ShapeDtypeStruct((index.shape[0], TILE, HEAD_DIM), bf16),
            in_specs=[smem(), vmem()],
            out_specs=vmem(),
            compiler_params=params(),
            name="pick",
        )(index, source)

    def same_core_exchange(x):
        x = x.reshape(chips, slots, TILE, HEAD_DIM)
        return lax.all_to_all(x, "seq", 0, 0, tiled=True, axis_index_groups=same_core)

    arrived = same_core_exchange(pick(block_of, tiles))
    arrived, gate1, up1, down1 = lax.optimization_barrier((arrived, gate1, up1, down1))
    arrived = arrived.reshape(z_count, heads, slots, TILE, HEAD_DIM)
    work = z_count * slots * TILE
    hid = 2 * gate0.shape[1]
    scaled = pl.pallas_call(
        scale_kernel,
        out_shape=jax.ShapeDtypeStruct((tp_count, work + 2 * TILE, width), bf16),
        in_specs=[vmem()] * 2,
        out_specs=vmem(),
        compiler_params=params(),
        name="scale",
    )(arrived, gain)
    scaled = lax.all_to_all(scaled, "tp", 0, 0, tiled=True)

    def run_hidden(*refs):
        hidden_kernel(width * tp_count, *refs)

    hidden = pl.pallas_call(
        run_hidden,
        out_shape=jax.ShapeDtypeStruct((work, hid), bf16),
        in_specs=[vmem()] * 5,
        out_specs=vmem(),
        compiler_params=params(),
        name="hidden",
    )(scaled, gate0, gate1, up0, up1)
    hidden = lax.all_gather(hidden, "tp")
    branch = pl.pallas_call(
        branch_kernel,
        out_shape=jax.ShapeDtypeStruct((z_count, heads, slots, TILE, HEAD_DIM), bf16),
        in_specs=[vmem()] * 3,
        out_specs=vmem(),
        compiler_params=params(),
        name="branch",
    )(hidden, down0, down1)
    returned = same_core_exchange(branch).reshape(chips * slots, TILE, HEAD_DIM)
    finished = lax.all_to_all(pick(slot_of, returned), "seq", 0, 0, tiled=True)
    return pl.pallas_call(
        finish_kernel,
        out_shape=jax.ShapeDtypeStruct((rows, width), bf16),
        in_specs=[vmem()] * 2,
        out_specs=vmem(),
        compiler_params=params(),
        name="finish",
    )(home, finished.reshape(stream.shape))


def solution(mesh):
    in_specs = (
        P("seq", "tp"),
        P("seq", "tp"),
        P("seq", "tp"),
        P("seq", "tp"),
        P(),
        P(),
        P("seq", None, "tp"),
        P("seq", None, "tp"),
        P("seq", None, "tp"),
    )
    out_specs = P("seq", "tp")
    return jax.shard_map(local, mesh=mesh, in_specs=in_specs, out_specs=out_specs, check_vma=False)
```

```python
import math

import jax
import jax.numpy as jnp
from jax import lax
from jax.experimental import pallas as pl
from jax.experimental.pallas import tpu as pltpu
from jax.sharding import PartitionSpec as P

HEAD_DIM = 128
BLOCK = 128
WINDOW = 512
TILE = 8

epsilon = 1e-05
masked_score = -1e30
f32 = jnp.float32
bf16 = jnp.bfloat16

VMEM_LIMIT = 14 * 1024 * 1024


def params():
    return pltpu.CompilerParams(vmem_limit_bytes=VMEM_LIMIT)


def vmem():
    return pl.BlockSpec(memory_space=pltpu.VMEM)


def smem():
    return pl.BlockSpec(memory_space=pltpu.SMEM)


def dot(a, b):
    return lax.dot_general(a, b, (((1,), (0,)), ((), ())), preferred_element_type=f32)


def dot_t(a, b):
    return lax.dot_general(a, b, (((1,), (1,)), ((), ())), preferred_element_type=f32)


def attend_near_kernel(place, q, kv0, kv1, kvx1, _, held, stats):
    row = lax.broadcasted_iota(jnp.int32, (BLOCK, BLOCK), 0)
    col = lax.broadcasted_iota(jnp.int32, (BLOCK, BLOCK), 1)
    diff = col - row
    shift1 = jnp.where(place[0] >= 1, 0, jnp.int32(4 * BLOCK))
    past = diff + BLOCK > shift1
    visible = jnp.concatenate([past, past, diff <= 0], axis=1)
    ones = jnp.ones((3 * BLOCK, HEAD_DIM), bf16)
    for h in range(q.shape[1] // HEAD_DIM):
        s = slice(h * HEAD_DIM, (h + 1) * HEAD_DIM)
        keys = jnp.concatenate([kv[:BLOCK, s] for kv in (kv1, kvx1, kv0)], axis=0)
        values = jnp.concatenate([kv[BLOCK:, s] for kv in (kv1, kvx1, kv0)], axis=0)
        scores = dot_t(q[:, s], keys) * (1.0 / math.sqrt(HEAD_DIM))
        scores = jnp.where(visible, scores, masked_score)
        top = jnp.max(scores, axis=1, keepdims=True)
        expo = jnp.exp(scores - top).astype(bf16)
        both = dot(expo, jnp.concatenate([values, ones], axis=1))
        held[:, s] = both[:, :HEAD_DIM]
        stats[0, :, s] = jnp.broadcast_to(top, (BLOCK, HEAD_DIM))
        stats[1, :, s] = both[:, HEAD_DIM:]


def attend_far_kernel(place, q, kv2, kvx0, kvx2, held, stats, res, out, home):
    chip = place[0]
    core = place[1]
    row = lax.broadcasted_iota(jnp.int32, (BLOCK, BLOCK), 0)
    col = lax.broadcasted_iota(jnp.int32, (BLOCK, BLOCK), 1)
    diff = col - row
    big = jnp.int32(4 * BLOCK)
    shift2 = jnp.where(chip >= 2, 0, big)
    shiftx = jnp.where((chip >= 2) | (core == 1), 0, big)
    seen2 = diff > shift2
    seenx = diff + BLOCK > shiftx
    ones = jnp.ones((2 * BLOCK, HEAD_DIM), bf16)
    z_count, core_count = out.shape[0], out.shape[2]
    for h in range(q.shape[1] // HEAD_DIM):
        s = slice(h * HEAD_DIM, (h + 1) * HEAD_DIM)
        kvx = kvx0[:, s] + kvx2[:, s]
        keys = jnp.concatenate([kv2[:BLOCK, s], kvx[:BLOCK]], axis=0)
        values = jnp.concatenate([kv2[BLOCK:, s], kvx[BLOCK:]], axis=0)
        scores = dot_t(q[:, s], keys) * (1.0 / math.sqrt(HEAD_DIM))
        score2 = jnp.where(seen2, scores[:, :BLOCK], masked_score)
        scorex = jnp.where(seenx, scores[:, BLOCK:], masked_score)
        near_top = stats[0, :, s]
        top = jnp.max(jnp.maximum(score2, scorex), axis=1, keepdims=True)
        top = jnp.maximum(near_top, top)
        expo = jnp.concatenate([jnp.exp(score2 - top), jnp.exp(scorex - top)], axis=1)
        both = dot(expo.astype(bf16), jnp.concatenate([values, ones], axis=1))
        scale = jnp.exp(near_top - top)
        total = stats[1, :, s] * scale + both[:, HEAD_DIM:]
        summed = held[:, s] * scale + both[:, :HEAD_DIM]
        stream = res[:, s].astype(f32) + summed / total
        home[:, s] = stream.astype(bf16)
        out[:, h] = stream.reshape(z_count, core_count, TILE, HEAD_DIM).astype(bf16)


def pick_kernel(index, tiles, out):
    @pl.loop(0, out.shape[0], unroll=8)
    def _(i):
        out[i] = tiles[index[i]]


def project_kernel(tiles, gain, first0, first1, out, held):
    z_count, heads, slots = tiles.shape[:3]
    rows = z_count * slots * TILE
    squares = jnp.zeros((rows, HEAD_DIM), f32)
    for h in range(heads):
        value = tiles[:, h].astype(f32).reshape(rows, HEAD_DIM)
        squares = squares + value * value
        s = slice(h * HEAD_DIM, (h + 1) * HEAD_DIM)
        held[:, s] = (value * gain[:, s]).astype(bf16)
    high = squares.astype(bf16)
    low = (squares - high.astype(f32)).astype(bf16)
    ones = jnp.ones((TILE, HEAD_DIM), bf16)
    total = dot_t(ones, high) + dot_t(ones, low)
    total_high = total.astype(bf16).astype(f32)
    total_rows = jnp.concatenate([total_high, total - total_high], axis=0).astype(bf16)
    x = held[...]
    parts = out.shape[0]
    for t in range(parts):
        width = first0.shape[2]
        out[t, :rows, :width] = dot(x, first0[t]).astype(bf16)
        out[t, :rows, width:] = dot(x, first1[t]).astype(bf16)
        out[t, rows:, :rows] = total_rows
        out[t, rows:, rows:] = total_rows


def hidden_kernel(features, parts, out):
    count = parts.shape[0]
    rows, width = out.shape[1:]
    tail = parts.shape[1] - rows
    squares = parts[:, rows:, :rows].reshape(count * tail, rows)
    weight = jnp.full((count * tail, HEAD_DIM), 1.0 / TILE, bf16)
    square = lax.dot_general(
        squares, weight, (((0,), (0,)), ((), ())), preferred_element_type=f32
    )
    factor = lax.rsqrt(square * (1.0 / features) + epsilon)
    half = width // 2
    for k in range(2):
        sums = sum(
            parts[t, :rows, k * width : (k + 1) * width].astype(f32) for t in range(count)
        )
        gate = sums[:, :half] * factor
        up = sums[:, half:] * factor
        value = (gate / (1.0 + jnp.exp(-gate)) * up).astype(bf16)
        for t in range(count):
            out[t, :, k * half : (k + 1) * half] = value


def branch_kernel(hidden, down0, down1, out):
    count = hidden.shape[0]
    half = hidden.shape[2] // 2
    first = jnp.concatenate([hidden[t, :, :half] for t in range(count)], axis=1)
    second = jnp.concatenate([hidden[t, :, half:] for t in range(count)], axis=1)
    z_count, heads, slots = out.shape[:3]
    step = 2 * HEAD_DIM
    for s in range(0, heads * HEAD_DIM, step):
        value = dot(first, down0[:, s : s + step]) + dot(second, down1[:, s : s + step])
        for k in range(0, step, HEAD_DIM):
            part = value[:, k : k + HEAD_DIM].reshape(z_count, slots, TILE, HEAD_DIM)
            out[:, (s + k) // HEAD_DIM] = part.astype(bf16)


def finish_kernel(home, branch, out):
    for h in range(branch.shape[1]):
        s = slice(h * HEAD_DIM, (h + 1) * HEAD_DIM)
        value = branch[:, h].astype(f32).reshape(home.shape[0], HEAD_DIM)
        out[:, s] = (home[:, s].astype(f32) + value).astype(bf16)


def local(
    queries, keys, values, residual_in, norm_gain, routing, gate_weight, up_weight, down_weight
):
    seq_count = lax.axis_size("seq")
    tp_count = lax.axis_size("tp")
    seq_place = lax.axis_index("seq")
    tp_place = lax.axis_index("tp")
    chips = seq_count // 2
    rows, width = queries.shape
    heads = width // HEAD_DIM
    z_count = rows // (2 * TILE)
    slots = 4

    onward = [(i, i + 2) for i in range(seq_count - 2)]
    to_odd = [(i, i + 1) for i in range(0, seq_count, 2)]
    to_even = [(i + 1, i) for i in range(0, seq_count, 2)]
    swap = to_odd + to_even
    same_core = [[c + 2 * i for i in range(chips)] for c in (0, 1)]

    def move(x, route):
        return lax.ppermute(x, "seq", route)

    kv0 = jnp.concatenate([keys, values], axis=0)
    kv1 = move(kv0, onward)
    kv2 = move(kv1, onward)
    kvx0 = move(kv0, to_odd)
    kvx1 = move(kv1, swap)

    gate_own, up_own, down0, kv0 = lax.optimization_barrier(
        (gate_weight[0], up_weight[0], down_weight[0], kv0)
    )
    both = jnp.concatenate([gate_own, up_own], axis=1).reshape(tp_count, width, -1)
    first0 = lax.all_to_all(both, "tp", 0, 0, tiled=True)
    down1 = move(down0, swap)
    gain = lax.dynamic_slice_in_dim(norm_gain, tp_place * width, width)[None]

    expert = routing[:, 0]
    block_range = jnp.arange(seq_count, dtype=jnp.int32)
    same = expert[None, :] == expert[:, None]
    rank = jnp.sum(same & (block_range[None, :] < block_range[:, None]), axis=1, dtype=jnp.int32)
    slot_of = expert * slots + rank
    slot_range = jnp.arange(chips * slots, dtype=jnp.int32)
    block_of = jnp.sum(
        jnp.where(slot_range[:, None] == slot_of[None, :], block_range[None, :], 0),
        axis=1,
        dtype=jnp.int32,
    )
    place = jnp.stack([seq_place // 2, seq_place % 2]).astype(jnp.int32)

    place, block_of, slot_of, gain = lax.optimization_barrier((place, block_of, slot_of, gain))
    held, stats = pl.pallas_call(
        attend_near_kernel,
        out_shape=(
            jax.ShapeDtypeStruct((rows, width), f32),
            jax.ShapeDtypeStruct((2, rows, width), f32),
        ),
        in_specs=[smem()] + [vmem()] * 5,
        out_specs=(vmem(), vmem()),
        compiler_params=params(),
        name="attend_near",
    )(place, queries, kv0, kv1, kvx1, residual_in)
    kv2, held, stats = lax.optimization_barrier((kv2, held, stats))
    kvx2 = move(kv2, to_even)
    stream, home = pl.pallas_call(
        attend_far_kernel,
        out_shape=(
            jax.ShapeDtypeStruct((z_count, heads, 2, TILE, HEAD_DIM), bf16),
            jax.ShapeDtypeStruct((rows, width), bf16),
        ),
        in_specs=[smem()] + [vmem()] * 7,
        out_specs=(vmem(), vmem()),
        compiler_params=params(),
        name="attend_far",
    )(place, queries, kv2, kvx0, kvx2, held, stats, residual_in)
    stream, first0, down1 = lax.optimization_barrier((stream, first0, down1))

    tiles = lax.all_to_all(
        stream.reshape(seq_count, TILE, HEAD_DIM), "seq", 0, 0, tiled=True
    )

    def pick(index, source):
        return pl.pallas_call(
            pick_kernel,
            out_shape=jax.ShapeDtypeStruct((index.shape[0], TILE, HEAD_DIM), bf16),
            in_specs=[smem(), vmem()],
            out_specs=vmem(),
            compiler_params=params(),
            name="pick",
        )(index, source)

    def same_core_exchange(x):
        x = x.reshape(chips, slots, TILE, HEAD_DIM)
        return lax.all_to_all(x, "seq", 0, 0, tiled=True, axis_index_groups=same_core)

    tiles, first0 = lax.optimization_barrier((tiles, first0))
    first1 = move(first0, swap)
    arrived = same_core_exchange(pick(block_of, tiles))
    arrived = arrived.reshape(z_count, heads, slots, TILE, HEAD_DIM)
    work = z_count * slots * TILE
    hid = first0.shape[2]
    parts = pl.pallas_call(
        project_kernel,
        out_shape=jax.ShapeDtypeStruct((tp_count, work + 2 * TILE, 2 * hid), bf16),
        in_specs=[vmem()] * 4,
        out_specs=vmem(),
        scratch_shapes=[pltpu.VMEM((work, width), bf16)],
        compiler_params=params(),
        name="project",
    )(arrived, gain, first0, first1)
    parts = lax.all_to_all(parts, "tp", 0, 0, tiled=True)

    def run_hidden(parts_ref, out_ref):
        hidden_kernel(width * tp_count, parts_ref, out_ref)

    hidden = pl.pallas_call(
        run_hidden,
        out_shape=jax.ShapeDtypeStruct((tp_count, work, hid), bf16),
        in_specs=[vmem()],
        out_specs=vmem(),
        compiler_params=params(),
        name="hidden",
    )(parts)
    hidden = lax.all_to_all(hidden, "tp", 0, 0, tiled=True)
    branch = pl.pallas_call(
        branch_kernel,
        out_shape=jax.ShapeDtypeStruct((z_count, heads, slots, TILE, HEAD_DIM), bf16),
        in_specs=[vmem()] * 3,
        out_specs=vmem(),
        compiler_params=params(),
        name="branch",
    )(hidden, down0, down1)
    returned = same_core_exchange(branch).reshape(chips * slots, TILE, HEAD_DIM)
    finished = lax.all_to_all(pick(slot_of, returned), "seq", 0, 0, tiled=True)
    return pl.pallas_call(
        finish_kernel,
        out_shape=jax.ShapeDtypeStruct((rows, width), bf16),
        in_specs=[vmem()] * 2,
        out_specs=vmem(),
        compiler_params=params(),
        name="finish",
    )(home, finished.reshape(stream.shape))


def solution(mesh):
    in_specs = (
        P("seq", "tp"),
        P("seq", "tp"),
        P("seq", "tp"),
        P("seq", "tp"),
        P(),
        P(),
        P("seq", None, "tp"),
        P("seq", None, "tp"),
        P("seq", None, "tp"),
    )
    out_specs = P("seq", "tp")
    return jax.shard_map(local, mesh=mesh, in_specs=in_specs, out_specs=out_specs, check_vma=False)
```

```python
import math

import jax
import jax.numpy as jnp
from jax import lax
from jax.experimental import pallas as pl
from jax.experimental.pallas import tpu as pltpu
from jax.sharding import PartitionSpec as P

HEAD_DIM = 128
BLOCK = 128
WINDOW = 512
TILE = 8

epsilon = 1e-05
masked_score = -1e30
f32 = jnp.float32
bf16 = jnp.bfloat16

VMEM_LIMIT = 14 * 1024 * 1024


def params():
    return pltpu.CompilerParams(vmem_limit_bytes=VMEM_LIMIT)


def vmem():
    return pl.BlockSpec(memory_space=pltpu.VMEM)


def smem():
    return pl.BlockSpec(memory_space=pltpu.SMEM)


def dot(a, b):
    return lax.dot_general(a, b, (((1,), (0,)), ((), ())), preferred_element_type=f32)


def dot_t(a, b):
    return lax.dot_general(a, b, (((1,), (1,)), ((), ())), preferred_element_type=f32)


def attend_near_kernel(place, q, kv0, kv1, _, held, stats):
    row = lax.broadcasted_iota(jnp.int32, (BLOCK, BLOCK), 0)
    col = lax.broadcasted_iota(jnp.int32, (BLOCK, BLOCK), 1)
    diff = col - row
    shift1 = jnp.where(place[0] >= 1, 0, jnp.int32(4 * BLOCK))
    past = diff + BLOCK > shift1
    visible = jnp.concatenate([past, diff <= 0], axis=1)
    ones = jnp.ones((2 * BLOCK, HEAD_DIM), bf16)
    for h in range(q.shape[1] // HEAD_DIM):
        s = slice(h * HEAD_DIM, (h + 1) * HEAD_DIM)
        keys = jnp.concatenate([kv[:BLOCK, s] for kv in (kv1, kv0)], axis=0)
        values = jnp.concatenate([kv[BLOCK:, s] for kv in (kv1, kv0)], axis=0)
        scores = dot_t(q[:, s], keys) * (1.0 / math.sqrt(HEAD_DIM))
        scores = jnp.where(visible, scores, masked_score)
        top = jnp.max(scores, axis=1, keepdims=True)
        expo = jnp.exp(scores - top).astype(bf16)
        both = dot(expo, jnp.concatenate([values, ones], axis=1))
        held[:, s] = both[:, :HEAD_DIM]
        stats[0, :, s] = jnp.broadcast_to(top, (BLOCK, HEAD_DIM))
        stats[1, :, s] = both[:, HEAD_DIM:]


def attend_far_kernel(place, q, kv2, kvx0, kvx1, kvx2, held, stats, res, out, home):
    chip = place[0]
    core = place[1]
    row = lax.broadcasted_iota(jnp.int32, (BLOCK, BLOCK), 0)
    col = lax.broadcasted_iota(jnp.int32, (BLOCK, BLOCK), 1)
    diff = col - row
    big = jnp.int32(4 * BLOCK)
    shift2 = jnp.where(chip >= 2, 0, big)
    shiftx = jnp.where((chip >= 2) | (core == 1), 0, big)
    seen2 = diff > shift2
    seenx = diff + BLOCK > shiftx
    seen1 = diff + BLOCK > jnp.where(chip >= 1, 0, big)
    ones = jnp.ones((3 * BLOCK, HEAD_DIM), bf16)
    z_count, core_count = out.shape[0], out.shape[2]
    for h in range(q.shape[1] // HEAD_DIM):
        s = slice(h * HEAD_DIM, (h + 1) * HEAD_DIM)
        kvx = kvx0[:, s] + kvx2[:, s]
        keys = jnp.concatenate([kv2[:BLOCK, s], kvx[:BLOCK], kvx1[:BLOCK, s]], axis=0)
        values = jnp.concatenate([kv2[BLOCK:, s], kvx[BLOCK:], kvx1[BLOCK:, s]], axis=0)
        scores = dot_t(q[:, s], keys) * (1.0 / math.sqrt(HEAD_DIM))
        score2 = jnp.where(seen2, scores[:, :BLOCK], masked_score)
        scorex = jnp.where(seenx, scores[:, BLOCK : 2 * BLOCK], masked_score)
        score1 = jnp.where(seen1, scores[:, 2 * BLOCK :], masked_score)
        near_top = stats[0, :, s]
        top = jnp.maximum(jnp.maximum(score2, scorex), score1)
        top = jnp.maximum(near_top, jnp.max(top, axis=1, keepdims=True))
        expo = jnp.concatenate([jnp.exp(part - top) for part in (score2, scorex, score1)], axis=1)
        both = dot(expo.astype(bf16), jnp.concatenate([values, ones], axis=1))
        scale = jnp.exp(near_top - top)
        total = stats[1, :, s] * scale + both[:, HEAD_DIM:]
        summed = held[:, s] * scale + both[:, :HEAD_DIM]
        stream = res[:, s].astype(f32) + summed / total
        home[:, s] = stream.astype(bf16)
        out[:, h] = stream.reshape(z_count, core_count, TILE, HEAD_DIM).astype(bf16)


def pick_kernel(index, tiles, out):
    @pl.loop(0, out.shape[0], unroll=8)
    def _(i):
        out[i] = tiles[index[i]]


def project_kernel(tiles, gain, first0, first1, out, held):
    z_count, heads, slots = tiles.shape[:3]
    rows = z_count * slots * TILE
    squares = jnp.zeros((rows, HEAD_DIM), f32)
    for h in range(heads):
        value = tiles[:, h].astype(f32).reshape(rows, HEAD_DIM)
        squares = squares + value * value
        s = slice(h * HEAD_DIM, (h + 1) * HEAD_DIM)
        held[:, s] = (value * gain[:, s]).astype(bf16)
    high = squares.astype(bf16)
    low = (squares - high.astype(f32)).astype(bf16)
    ones = jnp.ones((TILE, HEAD_DIM), bf16)
    total = dot_t(ones, high) + dot_t(ones, low)
    total_high = total.astype(bf16).astype(f32)
    total_rows = jnp.concatenate([total_high, total - total_high], axis=0).astype(bf16)
    x = held[...]
    parts = out.shape[0]
    for t in range(parts):
        width = first0.shape[2]
        out[t, :rows, :width] = dot(x, first0[t]).astype(bf16)
        out[t, :rows, width:] = dot(x, first1[t]).astype(bf16)
        out[t, rows:, :rows] = total_rows
        out[t, rows:, rows:] = total_rows


def hidden_kernel(features, parts, out):
    count = parts.shape[0]
    rows, width = out.shape[1:]
    tail = parts.shape[1] - rows
    squares = parts[:, rows:, :rows].reshape(count * tail, rows)
    weight = jnp.full((count * tail, HEAD_DIM), 1.0 / TILE, bf16)
    square = lax.dot_general(
        squares, weight, (((0,), (0,)), ((), ())), preferred_element_type=f32
    )
    factor = lax.rsqrt(square * (1.0 / features) + epsilon)
    half = width // 2
    for k in range(2):
        sums = sum(
            parts[t, :rows, k * width : (k + 1) * width].astype(f32) for t in range(count)
        )
        gate = sums[:, :half] * factor
        up = sums[:, half:] * factor
        value = (gate / (1.0 + jnp.exp(-gate)) * up).astype(bf16)
        for t in range(count):
            out[t, :, k * half : (k + 1) * half] = value


def branch_kernel(hidden, down0, down1, out):
    count = hidden.shape[0]
    half = hidden.shape[2] // 2
    first = jnp.concatenate([hidden[t, :, :half] for t in range(count)], axis=1)
    second = jnp.concatenate([hidden[t, :, half:] for t in range(count)], axis=1)
    z_count, heads, slots = out.shape[:3]
    step = 2 * HEAD_DIM
    for s in range(0, heads * HEAD_DIM, step):
        value = dot(first, down0[:, s : s + step]) + dot(second, down1[:, s : s + step])
        for k in range(0, step, HEAD_DIM):
            part = value[:, k : k + HEAD_DIM].reshape(z_count, slots, TILE, HEAD_DIM)
            out[:, (s + k) // HEAD_DIM] = part.astype(bf16)


def finish_kernel(home, branch, out):
    for h in range(branch.shape[1]):
        s = slice(h * HEAD_DIM, (h + 1) * HEAD_DIM)
        value = branch[:, h].astype(f32).reshape(home.shape[0], HEAD_DIM)
        out[:, s] = (home[:, s].astype(f32) + value).astype(bf16)


def local(
    queries, keys, values, residual_in, norm_gain, routing, gate_weight, up_weight, down_weight
):
    seq_count = lax.axis_size("seq")
    tp_count = lax.axis_size("tp")
    seq_place = lax.axis_index("seq")
    tp_place = lax.axis_index("tp")
    chips = seq_count // 2
    rows, width = queries.shape
    heads = width // HEAD_DIM
    z_count = rows // (2 * TILE)
    slots = 4

    onward = [(i, i + 2) for i in range(seq_count - 2)]
    to_odd = [(i, i + 1) for i in range(0, seq_count, 2)]
    to_even = [(i + 1, i) for i in range(0, seq_count, 2)]
    swap = to_odd + to_even
    same_core = [[c + 2 * i for i in range(chips)] for c in (0, 1)]

    def move(x, route):
        return lax.ppermute(x, "seq", route)

    kv0 = jnp.concatenate([keys, values], axis=0)
    kv1 = move(kv0, onward)
    kv2 = move(kv1, onward)
    kvx0 = move(kv0, to_odd)
    kvx1 = move(kv1, swap)

    gate_own, up_own, down0, kv0 = lax.optimization_barrier(
        (gate_weight[0], up_weight[0], down_weight[0], kv0)
    )
    both = jnp.concatenate([gate_own, up_own], axis=1).reshape(tp_count, width, -1)
    first0 = lax.all_to_all(both, "tp", 0, 0, tiled=True)
    down1 = move(down0, swap)
    gain = lax.dynamic_slice_in_dim(norm_gain, tp_place * width, width)[None]

    expert = routing[:, 0]
    block_range = jnp.arange(seq_count, dtype=jnp.int32)
    same = expert[None, :] == expert[:, None]
    rank = jnp.sum(same & (block_range[None, :] < block_range[:, None]), axis=1, dtype=jnp.int32)
    slot_of = expert * slots + rank
    slot_range = jnp.arange(chips * slots, dtype=jnp.int32)
    block_of = jnp.sum(
        jnp.where(slot_range[:, None] == slot_of[None, :], block_range[None, :], 0),
        axis=1,
        dtype=jnp.int32,
    )
    place = jnp.stack([seq_place // 2, seq_place % 2]).astype(jnp.int32)

    place, block_of, slot_of, gain = lax.optimization_barrier((place, block_of, slot_of, gain))
    held, stats = pl.pallas_call(
        attend_near_kernel,
        out_shape=(
            jax.ShapeDtypeStruct((rows, width), f32),
            jax.ShapeDtypeStruct((2, rows, width), f32),
        ),
        in_specs=[smem()] + [vmem()] * 4,
        out_specs=(vmem(), vmem()),
        compiler_params=params(),
        name="attend_near",
    )(place, queries, kv0, kv1, residual_in)
    kv2, held, stats = lax.optimization_barrier((kv2, held, stats))
    kvx2 = move(kv2, to_even)
    stream, home = pl.pallas_call(
        attend_far_kernel,
        out_shape=(
            jax.ShapeDtypeStruct((z_count, heads, 2, TILE, HEAD_DIM), bf16),
            jax.ShapeDtypeStruct((rows, width), bf16),
        ),
        in_specs=[smem()] + [vmem()] * 8,
        out_specs=(vmem(), vmem()),
        compiler_params=params(),
        name="attend_far",
    )(place, queries, kv2, kvx0, kvx1, kvx2, held, stats, residual_in)
    stream, first0, down1 = lax.optimization_barrier((stream, first0, down1))

    tiles = lax.all_to_all(
        stream.reshape(seq_count, TILE, HEAD_DIM), "seq", 0, 0, tiled=True
    )

    def pick(index, source):
        return pl.pallas_call(
            pick_kernel,
            out_shape=jax.ShapeDtypeStruct((index.shape[0], TILE, HEAD_DIM), bf16),
            in_specs=[smem(), vmem()],
            out_specs=vmem(),
            compiler_params=params(),
            name="pick",
        )(index, source)

    def same_core_exchange(x):
        x = x.reshape(chips, slots, TILE, HEAD_DIM)
        return lax.all_to_all(x, "seq", 0, 0, tiled=True, axis_index_groups=same_core)

    tiles, first0 = lax.optimization_barrier((tiles, first0))
    first1 = move(first0, swap)
    arrived = same_core_exchange(pick(block_of, tiles))
    arrived = arrived.reshape(z_count, heads, slots, TILE, HEAD_DIM)
    work = z_count * slots * TILE
    hid = first0.shape[2]
    parts = pl.pallas_call(
        project_kernel,
        out_shape=jax.ShapeDtypeStruct((tp_count, work + 2 * TILE, 2 * hid), bf16),
        in_specs=[vmem()] * 4,
        out_specs=vmem(),
        scratch_shapes=[pltpu.VMEM((work, width), bf16)],
        compiler_params=params(),
        name="project",
    )(arrived, gain, first0, first1)
    parts = lax.all_to_all(parts, "tp", 0, 0, tiled=True)

    def run_hidden(parts_ref, out_ref):
        hidden_kernel(width * tp_count, parts_ref, out_ref)

    hidden = pl.pallas_call(
        run_hidden,
        out_shape=jax.ShapeDtypeStruct((tp_count, work, hid), bf16),
        in_specs=[vmem()],
        out_specs=vmem(),
        compiler_params=params(),
        name="hidden",
    )(parts)
    hidden = lax.all_to_all(hidden, "tp", 0, 0, tiled=True)
    branch = pl.pallas_call(
        branch_kernel,
        out_shape=jax.ShapeDtypeStruct((z_count, heads, slots, TILE, HEAD_DIM), bf16),
        in_specs=[vmem()] * 3,
        out_specs=vmem(),
        compiler_params=params(),
        name="branch",
    )(hidden, down0, down1)
    returned = same_core_exchange(branch).reshape(chips * slots, TILE, HEAD_DIM)
    finished = lax.all_to_all(pick(slot_of, returned), "seq", 0, 0, tiled=True)
    return pl.pallas_call(
        finish_kernel,
        out_shape=jax.ShapeDtypeStruct((rows, width), bf16),
        in_specs=[vmem()] * 2,
        out_specs=vmem(),
        compiler_params=params(),
        name="finish",
    )(home, finished.reshape(stream.shape))


def solution(mesh):
    in_specs = (
        P("seq", "tp"),
        P("seq", "tp"),
        P("seq", "tp"),
        P("seq", "tp"),
        P(),
        P(),
        P("seq", None, "tp"),
        P("seq", None, "tp"),
        P("seq", None, "tp"),
    )
    out_specs = P("seq", "tp")
    return jax.shard_map(local, mesh=mesh, in_specs=in_specs, out_specs=out_specs, check_vma=False)
```

```python
import math

import jax
import jax.numpy as jnp
from jax import lax
from jax.experimental import pallas as pl
from jax.experimental.pallas import tpu as pltpu
from jax.sharding import PartitionSpec as P

HEAD_DIM = 128
BLOCK = 128
WINDOW = 512
TILE = 8

epsilon = 1e-05
masked_score = -1e30
f32 = jnp.float32
bf16 = jnp.bfloat16

VMEM_LIMIT = 14 * 1024 * 1024


def params():
    return pltpu.CompilerParams(vmem_limit_bytes=VMEM_LIMIT)


def vmem():
    return pl.BlockSpec(memory_space=pltpu.VMEM)


def smem():
    return pl.BlockSpec(memory_space=pltpu.SMEM)


def dot(a, b):
    return lax.dot_general(a, b, (((1,), (0,)), ((), ())), preferred_element_type=f32)


def dot_t(a, b):
    return lax.dot_general(a, b, (((1,), (1,)), ((), ())), preferred_element_type=f32)


def attend_near_kernel(place, q, kv0, kv1, _, held, stats):
    row = lax.broadcasted_iota(jnp.int32, (BLOCK, BLOCK), 0)
    col = lax.broadcasted_iota(jnp.int32, (BLOCK, BLOCK), 1)
    diff = col - row
    shift1 = jnp.where(place[0] >= 1, 0, jnp.int32(4 * BLOCK))
    past = diff + BLOCK > shift1
    visible = jnp.concatenate([past, diff <= 0], axis=1)
    ones = jnp.ones((2 * BLOCK, HEAD_DIM), bf16)
    for h in range(q.shape[1] // HEAD_DIM):
        s = slice(h * HEAD_DIM, (h + 1) * HEAD_DIM)
        keys = jnp.concatenate([kv[:BLOCK, s] for kv in (kv1, kv0)], axis=0)
        values = jnp.concatenate([kv[BLOCK:, s] for kv in (kv1, kv0)], axis=0)
        scores = dot_t(q[:, s], keys) * (1.0 / math.sqrt(HEAD_DIM))
        scores = jnp.where(visible, scores, masked_score)
        top = jnp.max(scores, axis=1, keepdims=True)
        expo = jnp.exp(scores - top).astype(bf16)
        both = dot(expo, jnp.concatenate([values, ones], axis=1))
        held[:, s] = both[:, :HEAD_DIM]
        stats[0, :, s] = jnp.broadcast_to(top, (BLOCK, HEAD_DIM))
        stats[1, :, s] = both[:, HEAD_DIM:]


def attend_far_kernel(place, q, kv2, kvx0, kvx1, kvx2, held, stats, res, out, home):
    chip = place[0]
    core = place[1]
    row = lax.broadcasted_iota(jnp.int32, (BLOCK, BLOCK), 0)
    col = lax.broadcasted_iota(jnp.int32, (BLOCK, BLOCK), 1)
    diff = col - row
    big = jnp.int32(4 * BLOCK)
    shift2 = jnp.where(chip >= 2, 0, big)
    shiftx = jnp.where((chip >= 2) | (core == 1), 0, big)
    seen2 = diff > shift2
    seenx = diff + BLOCK > shiftx
    seen1 = diff + BLOCK > jnp.where(chip >= 1, 0, big)
    ones = jnp.ones((3 * BLOCK, HEAD_DIM), bf16)
    z_count, core_count = out.shape[0], out.shape[2]
    for h in range(q.shape[1] // HEAD_DIM):
        s = slice(h * HEAD_DIM, (h + 1) * HEAD_DIM)
        kvx = kvx0[:, s] + kvx2[:, s]
        keys = jnp.concatenate([kv2[:BLOCK, s], kvx[:BLOCK], kvx1[:BLOCK, s]], axis=0)
        values = jnp.concatenate([kv2[BLOCK:, s], kvx[BLOCK:], kvx1[BLOCK:, s]], axis=0)
        scores = dot_t(q[:, s], keys) * (1.0 / math.sqrt(HEAD_DIM))
        score2 = jnp.where(seen2, scores[:, :BLOCK], masked_score)
        scorex = jnp.where(seenx, scores[:, BLOCK : 2 * BLOCK], masked_score)
        score1 = jnp.where(seen1, scores[:, 2 * BLOCK :], masked_score)
        near_top = stats[0, :, s]
        top = jnp.maximum(jnp.maximum(score2, scorex), score1)
        top = jnp.maximum(near_top, jnp.max(top, axis=1, keepdims=True))
        expo = jnp.concatenate([jnp.exp(part - top) for part in (score2, scorex, score1)], axis=1)
        both = dot(expo.astype(bf16), jnp.concatenate([values, ones], axis=1))
        scale = jnp.exp(near_top - top)
        total = stats[1, :, s] * scale + both[:, HEAD_DIM:]
        summed = held[:, s] * scale + both[:, :HEAD_DIM]
        stream = res[:, s].astype(f32) + summed / total
        home[:, s] = stream.astype(bf16)
        out[:, h] = stream.reshape(z_count, core_count, TILE, HEAD_DIM).astype(bf16)


def pick_kernel(index, tiles, out):
    @pl.loop(0, out.shape[0], unroll=32)
    def _(i):
        out[i] = tiles[index[i]]


def project_kernel(tiles, gain, first0, first1, out, held):
    z_count, heads, slots = tiles.shape[:3]
    rows = z_count * slots * TILE
    squares = jnp.zeros((rows, HEAD_DIM), f32)
    for h in range(heads):
        value = tiles[:, h].astype(f32).reshape(rows, HEAD_DIM)
        squares = squares + value * value
        s = slice(h * HEAD_DIM, (h + 1) * HEAD_DIM)
        held[:, s] = (value * gain[:, s]).astype(bf16)
    high = squares.astype(bf16)
    low = (squares - high.astype(f32)).astype(bf16)
    ones = jnp.ones((TILE, HEAD_DIM), bf16)
    total = dot_t(ones, high) + dot_t(ones, low)
    total_high = total.astype(bf16).astype(f32)
    total_rows = jnp.concatenate([total_high, total - total_high], axis=0).astype(bf16)
    x = held[...]
    parts = out.shape[0]
    for t in range(parts):
        width = first0.shape[2]
        out[t, :rows, :width] = dot(x, first0[t]).astype(bf16)
        out[t, :rows, width:] = dot(x, first1[t]).astype(bf16)
        out[t, rows:, :rows] = total_rows
        out[t, rows:, rows:] = total_rows


def hidden_kernel(features, parts, out):
    count = parts.shape[0]
    rows, width = out.shape[1:]
    tail = parts.shape[1] - rows
    squares = parts[:, rows:, :rows].reshape(count * tail, rows)
    weight = jnp.full((count * tail, HEAD_DIM), 1.0 / TILE, bf16)
    square = lax.dot_general(
        squares, weight, (((0,), (0,)), ((), ())), preferred_element_type=f32
    )
    factor = lax.rsqrt(square * (1.0 / features) + epsilon)
    half = width // 2
    for k in range(2):
        sums = sum(
            parts[t, :rows, k * width : (k + 1) * width].astype(f32) for t in range(count)
        )
        gate = sums[:, :half] * factor
        up = sums[:, half:] * factor
        value = (gate / (1.0 + jnp.exp(-gate)) * up).astype(bf16)
        for t in range(count):
            out[t, :, k * half : (k + 1) * half] = value


def branch_kernel(hidden, down0, down1, out, total, held, sem):
    copy = pltpu.make_async_copy(down1, held, sem)
    copy.start()
    count = hidden.shape[0]
    half = hidden.shape[2] // 2
    first = jnp.concatenate([hidden[t, :, :half] for t in range(count)], axis=1)
    second = jnp.concatenate([hidden[t, :, half:] for t in range(count)], axis=1)
    z_count, heads, slots = out.shape[:3]
    step = 2 * HEAD_DIM
    for s in range(0, heads * HEAD_DIM, step):
        total[:, s : s + step] = dot(first, down0[:, s : s + step])
    copy.wait()
    for s in range(0, heads * HEAD_DIM, step):
        value = total[:, s : s + step] + dot(second, held[:, s : s + step])
        for k in range(0, step, HEAD_DIM):
            part = value[:, k : k + HEAD_DIM].reshape(z_count, slots, TILE, HEAD_DIM)
            out[:, (s + k) // HEAD_DIM] = part.astype(bf16)


def finish_kernel(home, branch, out):
    for h in range(branch.shape[1]):
        s = slice(h * HEAD_DIM, (h + 1) * HEAD_DIM)
        value = branch[:, h].astype(f32).reshape(home.shape[0], HEAD_DIM)
        out[:, s] = (home[:, s].astype(f32) + value).astype(bf16)


def local(
    queries, keys, values, residual_in, norm_gain, routing, gate_weight, up_weight, down_weight
):
    seq_count = lax.axis_size("seq")
    tp_count = lax.axis_size("tp")
    seq_place = lax.axis_index("seq")
    tp_place = lax.axis_index("tp")
    chips = seq_count // 2
    rows, width = queries.shape
    heads = width // HEAD_DIM
    z_count = rows // (2 * TILE)
    slots = 4

    onward = [(i, i + 2) for i in range(seq_count - 2)]
    to_odd = [(i, i + 1) for i in range(0, seq_count, 2)]
    to_even = [(i + 1, i) for i in range(0, seq_count, 2)]
    swap = to_odd + to_even
    same_core = [[c + 2 * i for i in range(chips)] for c in (0, 1)]

    def move(x, route):
        return lax.ppermute(x, "seq", route)

    kv0 = jnp.concatenate([keys, values], axis=0)
    kv1 = move(kv0, onward)
    kv2 = move(kv1, onward)
    kvx0 = move(kv0, to_odd)
    kvx1 = move(kv1, swap)

    gate_own, up_own, down0, kv0 = lax.optimization_barrier(
        (gate_weight[0], up_weight[0], down_weight[0], kv0)
    )
    both = jnp.concatenate([gate_own, up_own], axis=1).reshape(tp_count, width, -1)
    first0 = lax.all_to_all(both, "tp", 0, 0, tiled=True)
    down1 = move(down0, swap)
    gain = lax.dynamic_slice_in_dim(norm_gain, tp_place * width, width)[None]

    expert = routing[:, 0]
    block_range = jnp.arange(seq_count, dtype=jnp.int32)
    same = expert[None, :] == expert[:, None]
    rank = jnp.sum(same & (block_range[None, :] < block_range[:, None]), axis=1, dtype=jnp.int32)
    slot_of = expert * slots + rank
    slot_range = jnp.arange(chips * slots, dtype=jnp.int32)
    block_of = jnp.sum(
        jnp.where(slot_range[:, None] == slot_of[None, :], block_range[None, :], 0),
        axis=1,
        dtype=jnp.int32,
    )
    place = jnp.stack([seq_place // 2, seq_place % 2]).astype(jnp.int32)

    place, block_of, slot_of, gain = lax.optimization_barrier((place, block_of, slot_of, gain))
    held, stats = pl.pallas_call(
        attend_near_kernel,
        out_shape=(
            jax.ShapeDtypeStruct((rows, width), f32),
            jax.ShapeDtypeStruct((2, rows, width), f32),
        ),
        in_specs=[smem()] + [vmem()] * 4,
        out_specs=(vmem(), vmem()),
        compiler_params=params(),
        name="attend_near",
    )(place, queries, kv0, kv1, residual_in)
    kv2, held, stats = lax.optimization_barrier((kv2, held, stats))
    kvx2 = move(kv2, to_even)
    stream, home = pl.pallas_call(
        attend_far_kernel,
        out_shape=(
            jax.ShapeDtypeStruct((z_count, heads, 2, TILE, HEAD_DIM), bf16),
            jax.ShapeDtypeStruct((rows, width), bf16),
        ),
        in_specs=[smem()] + [vmem()] * 8,
        out_specs=(vmem(), vmem()),
        compiler_params=params(),
        name="attend_far",
    )(place, queries, kv2, kvx0, kvx1, kvx2, held, stats, residual_in)
    stream, first0, down1 = lax.optimization_barrier((stream, first0, down1))

    tiles = lax.all_to_all(
        stream.reshape(seq_count, TILE, HEAD_DIM), "seq", 0, 0, tiled=True
    )

    def pick(index, source):
        return pl.pallas_call(
            pick_kernel,
            out_shape=jax.ShapeDtypeStruct((index.shape[0], TILE, HEAD_DIM), bf16),
            in_specs=[smem(), vmem()],
            out_specs=vmem(),
            compiler_params=params(),
            name="pick",
        )(index, source)

    def same_core_exchange(x):
        x = x.reshape(chips, slots, TILE, HEAD_DIM)
        return lax.all_to_all(x, "seq", 0, 0, tiled=True, axis_index_groups=same_core)

    tiles, first0 = lax.optimization_barrier((tiles, first0))
    first1 = move(first0, swap)
    arrived = same_core_exchange(pick(block_of, tiles))
    arrived = arrived.reshape(z_count, heads, slots, TILE, HEAD_DIM)
    work = z_count * slots * TILE
    hid = first0.shape[2]
    parts = pl.pallas_call(
        project_kernel,
        out_shape=jax.ShapeDtypeStruct((tp_count, work + 2 * TILE, 2 * hid), bf16),
        in_specs=[vmem()] * 4,
        out_specs=vmem(),
        scratch_shapes=[pltpu.VMEM((work, width), bf16)],
        compiler_params=params(),
        name="project",
    )(arrived, gain, first0, first1)
    parts = lax.all_to_all(parts, "tp", 0, 0, tiled=True)

    def run_hidden(parts_ref, out_ref):
        hidden_kernel(width * tp_count, parts_ref, out_ref)

    hidden = pl.pallas_call(
        run_hidden,
        out_shape=jax.ShapeDtypeStruct((tp_count, work, hid), bf16),
        in_specs=[vmem()],
        out_specs=vmem(),
        compiler_params=params(),
        name="hidden",
    )(parts)
    hidden = lax.all_to_all(hidden, "tp", 0, 0, tiled=True)
    branch = pl.pallas_call(
        branch_kernel,
        out_shape=jax.ShapeDtypeStruct((z_count, heads, slots, TILE, HEAD_DIM), bf16),
        in_specs=[vmem(), vmem(), pl.BlockSpec(memory_space=pl.ANY)],
        out_specs=vmem(),
        scratch_shapes=[
            pltpu.VMEM((work, width), f32),
            pltpu.VMEM(down1.shape, bf16),
            pltpu.SemaphoreType.DMA,
        ],
        compiler_params=params(),
        name="branch",
    )(hidden, down0, down1)
    returned = same_core_exchange(branch).reshape(chips * slots, TILE, HEAD_DIM)
    finished = lax.all_to_all(pick(slot_of, returned), "seq", 0, 0, tiled=True)
    return pl.pallas_call(
        finish_kernel,
        out_shape=jax.ShapeDtypeStruct((rows, width), bf16),
        in_specs=[vmem()] * 2,
        out_specs=vmem(),
        compiler_params=params(),
        name="finish",
    )(home, finished.reshape(stream.shape))


def solution(mesh):
    in_specs = (
        P("seq", "tp"),
        P("seq", "tp"),
        P("seq", "tp"),
        P("seq", "tp"),
        P(),
        P(),
        P("seq", None, "tp"),
        P("seq", None, "tp"),
        P("seq", None, "tp"),
    )
    out_specs = P("seq", "tp")
    return jax.shard_map(local, mesh=mesh, in_specs=in_specs, out_specs=out_specs, check_vma=False)
```

```python
import math

import jax
import jax.numpy as jnp
from jax import lax
from jax.experimental import pallas as pl
from jax.experimental.pallas import tpu as pltpu
from jax.sharding import PartitionSpec as P

HEAD_DIM = 128
BLOCK = 128
WINDOW = 512
TILE = 8

epsilon = 1e-05
masked_score = -1e30
f32 = jnp.float32
bf16 = jnp.bfloat16

VMEM_LIMIT = 14 * 1024 * 1024


def params():
    return pltpu.CompilerParams(vmem_limit_bytes=VMEM_LIMIT)


def vmem():
    return pl.BlockSpec(memory_space=pltpu.VMEM)


def smem():
    return pl.BlockSpec(memory_space=pltpu.SMEM)


def dot(a, b):
    return lax.dot_general(a, b, (((1,), (0,)), ((), ())), preferred_element_type=f32)


def dot_t(a, b):
    return lax.dot_general(a, b, (((1,), (1,)), ((), ())), preferred_element_type=f32)


def join_kernel(first, second, out, sems):
    rows = first.shape[0]
    copies = [
        pltpu.make_async_copy(first, out.at[:rows], sems.at[0]),
        pltpu.make_async_copy(second, out.at[rows:], sems.at[1]),
    ]
    for copy in copies:
        copy.start()
    for copy in copies:
        copy.wait()


def attend_near_kernel(place, q, kv0, kv1, _, held, stats):
    row = lax.broadcasted_iota(jnp.int32, (BLOCK, BLOCK), 0)
    col = lax.broadcasted_iota(jnp.int32, (BLOCK, BLOCK), 1)
    diff = col - row
    shift1 = jnp.where(place[0] >= 1, 0, jnp.int32(4 * BLOCK))
    past = diff + BLOCK > shift1
    visible = jnp.concatenate([past, diff <= 0], axis=1)
    ones = jnp.ones((2 * BLOCK, HEAD_DIM), bf16)
    for h in range(q.shape[1] // HEAD_DIM):
        s = slice(h * HEAD_DIM, (h + 1) * HEAD_DIM)
        keys = jnp.concatenate([kv[:BLOCK, s] for kv in (kv1, kv0)], axis=0)
        values = jnp.concatenate([kv[BLOCK:, s] for kv in (kv1, kv0)], axis=0)
        scores = dot_t(q[:, s], keys) * (1.0 / math.sqrt(HEAD_DIM))
        scores = jnp.where(visible, scores, masked_score)
        top = jnp.max(scores, axis=1, keepdims=True)
        expo = jnp.exp(scores - top).astype(bf16)
        both = dot(expo, jnp.concatenate([values, ones], axis=1))
        held[:, s] = both[:, :HEAD_DIM]
        stats[0, :, s] = jnp.broadcast_to(top, (BLOCK, HEAD_DIM))
        stats[1, :, s] = both[:, HEAD_DIM:]


def attend_far_kernel(place, q, kv2, kvx0, kvx1, kvx2, held, stats, res, out, home):
    chip = place[0]
    core = place[1]
    row = lax.broadcasted_iota(jnp.int32, (BLOCK, BLOCK), 0)
    col = lax.broadcasted_iota(jnp.int32, (BLOCK, BLOCK), 1)
    diff = col - row
    big = jnp.int32(4 * BLOCK)
    shift2 = jnp.where(chip >= 2, 0, big)
    shiftx = jnp.where((chip >= 2) | (core == 1), 0, big)
    seen2 = diff > shift2
    seenx = diff + BLOCK > shiftx
    seen1 = diff + BLOCK > jnp.where(chip >= 1, 0, big)
    ones = jnp.ones((3 * BLOCK, HEAD_DIM), bf16)
    z_count, core_count = out.shape[0], out.shape[2]
    for h in range(q.shape[1] // HEAD_DIM):
        s = slice(h * HEAD_DIM, (h + 1) * HEAD_DIM)
        kvx = kvx0[:, s] + kvx2[:, s]
        keys = jnp.concatenate([kv2[:BLOCK, s], kvx[:BLOCK], kvx1[:BLOCK, s]], axis=0)
        values = jnp.concatenate([kv2[BLOCK:, s], kvx[BLOCK:], kvx1[BLOCK:, s]], axis=0)
        scores = dot_t(q[:, s], keys) * (1.0 / math.sqrt(HEAD_DIM))
        score2 = jnp.where(seen2, scores[:, :BLOCK], masked_score)
        scorex = jnp.where(seenx, scores[:, BLOCK : 2 * BLOCK], masked_score)
        score1 = jnp.where(seen1, scores[:, 2 * BLOCK :], masked_score)
        near_top = stats[0, :, s]
        top = jnp.maximum(jnp.maximum(score2, scorex), score1)
        top = jnp.maximum(near_top, jnp.max(top, axis=1, keepdims=True))
        expo = jnp.concatenate([jnp.exp(part - top) for part in (score2, scorex, score1)], axis=1)
        both = dot(expo.astype(bf16), jnp.concatenate([values, ones], axis=1))
        scale = jnp.exp(near_top - top)
        total = stats[1, :, s] * scale + both[:, HEAD_DIM:]
        summed = held[:, s] * scale + both[:, :HEAD_DIM]
        stream = res[:, s].astype(f32) + summed / total
        home[:, s] = stream.astype(bf16)
        out[:, h] = stream.reshape(z_count, core_count, TILE, HEAD_DIM).astype(bf16)


def pick_kernel(index, tiles, out):
    @pl.loop(0, out.shape[0], unroll=32)
    def _(i):
        out[i] = tiles[index[i]]


def project_kernel(tiles, gain, first0, first1, out, held):
    z_count, heads, slots = tiles.shape[:3]
    rows = z_count * slots * TILE
    squares = jnp.zeros((rows, HEAD_DIM), f32)
    for h in range(heads):
        value = tiles[:, h].astype(f32).reshape(rows, HEAD_DIM)
        squares = squares + value * value
        s = slice(h * HEAD_DIM, (h + 1) * HEAD_DIM)
        held[:, s] = (value * gain[:, s]).astype(bf16)
    high = squares.astype(bf16)
    low = (squares - high.astype(f32)).astype(bf16)
    ones = jnp.ones((TILE, HEAD_DIM), bf16)
    total = dot_t(ones, high) + dot_t(ones, low)
    total_high = total.astype(bf16).astype(f32)
    total_rows = jnp.concatenate([total_high, total - total_high], axis=0).astype(bf16)
    x = held[...]
    parts = out.shape[0]
    for t in range(parts):
        width = first0.shape[2]
        out[t, :rows, :width] = dot(x, first0[t]).astype(bf16)
        out[t, :rows, width:] = dot(x, first1[t]).astype(bf16)
        out[t, rows:, :rows] = total_rows
        out[t, rows:, rows:] = total_rows


def hidden_kernel(features, parts, out):
    count = parts.shape[0]
    rows, width = out.shape[1:]
    tail = parts.shape[1] - rows
    squares = parts[:, rows:, :rows].reshape(count * tail, rows)
    weight = jnp.full((count * tail, HEAD_DIM), 1.0 / TILE, bf16)
    square = lax.dot_general(
        squares, weight, (((0,), (0,)), ((), ())), preferred_element_type=f32
    )
    factor = lax.rsqrt(square * (1.0 / features) + epsilon)
    half = width // 2
    for k in range(2):
        sums = sum(
            parts[t, :rows, k * width : (k + 1) * width].astype(f32) for t in range(count)
        )
        gate = sums[:, :half] * factor
        up = sums[:, half:] * factor
        value = (gate / (1.0 + jnp.exp(-gate)) * up).astype(bf16)
        for t in range(count):
            out[t, :, k * half : (k + 1) * half] = value


def branch_kernel(hidden, down0, down1, out, total, held, sem):
    copy = pltpu.make_async_copy(down1, held, sem)
    copy.start()
    count = hidden.shape[0]
    half = hidden.shape[2] // 2
    first = jnp.concatenate([hidden[t, :, :half] for t in range(count)], axis=1)
    second = jnp.concatenate([hidden[t, :, half:] for t in range(count)], axis=1)
    z_count, heads, slots = out.shape[:3]
    step = 2 * HEAD_DIM
    for s in range(0, heads * HEAD_DIM, step):
        total[:, s : s + step] = dot(first, down0[:, s : s + step])
    copy.wait()
    for s in range(0, heads * HEAD_DIM, step):
        value = total[:, s : s + step] + dot(second, held[:, s : s + step])
        for k in range(0, step, HEAD_DIM):
            part = value[:, k : k + HEAD_DIM].reshape(z_count, slots, TILE, HEAD_DIM)
            out[:, (s + k) // HEAD_DIM] = part.astype(bf16)


def finish_kernel(home, branch, out):
    for h in range(branch.shape[1]):
        s = slice(h * HEAD_DIM, (h + 1) * HEAD_DIM)
        value = branch[:, h].astype(f32).reshape(home.shape[0], HEAD_DIM)
        out[:, s] = (home[:, s].astype(f32) + value).astype(bf16)


def local(
    queries, keys, values, residual_in, norm_gain, routing, gate_weight, up_weight, down_weight
):
    seq_count = lax.axis_size("seq")
    tp_count = lax.axis_size("tp")
    seq_place = lax.axis_index("seq")
    tp_place = lax.axis_index("tp")
    chips = seq_count // 2
    rows, width = queries.shape
    heads = width // HEAD_DIM
    z_count = rows // (2 * TILE)
    slots = 4

    onward = [(i, i + 2) for i in range(seq_count - 2)]
    to_odd = [(i, i + 1) for i in range(0, seq_count, 2)]
    to_even = [(i + 1, i) for i in range(0, seq_count, 2)]
    swap = to_odd + to_even
    same_core = [[c + 2 * i for i in range(chips)] for c in (0, 1)]

    def move(x, route):
        return lax.ppermute(x, "seq", route)

    kv0 = pl.pallas_call(
        join_kernel,
        out_shape=jax.ShapeDtypeStruct((2 * rows, width), bf16),
        in_specs=[pl.BlockSpec(memory_space=pl.ANY)] * 2,
        out_specs=vmem(),
        scratch_shapes=[pltpu.SemaphoreType.DMA((2,))],
        compiler_params=pltpu.CompilerParams(vmem_limit_bytes=56 * 1024 * 1024),
        name="join",
    )(keys, values)
    kv1 = move(kv0, onward)
    kv2 = move(kv1, onward)
    kvx0 = move(kv0, to_odd)
    kvx1 = move(kv1, swap)

    gate_own, up_own, down0, kv0 = lax.optimization_barrier(
        (gate_weight[0], up_weight[0], down_weight[0], kv0)
    )
    both = jnp.concatenate([gate_own, up_own], axis=1).reshape(tp_count, width, -1)
    first0 = lax.all_to_all(both, "tp", 0, 0, tiled=True)
    down1 = move(down0, swap)
    gain = lax.dynamic_slice_in_dim(norm_gain, tp_place * width, width)[None]

    expert = routing[:, 0]
    block_range = jnp.arange(seq_count, dtype=jnp.int32)
    same = expert[None, :] == expert[:, None]
    rank = jnp.sum(same & (block_range[None, :] < block_range[:, None]), axis=1, dtype=jnp.int32)
    slot_of = expert * slots + rank
    slot_range = jnp.arange(chips * slots, dtype=jnp.int32)
    block_of = jnp.sum(
        jnp.where(slot_range[:, None] == slot_of[None, :], block_range[None, :], 0),
        axis=1,
        dtype=jnp.int32,
    )
    place = jnp.stack([seq_place // 2, seq_place % 2]).astype(jnp.int32)

    place, block_of, slot_of, gain = lax.optimization_barrier((place, block_of, slot_of, gain))
    held, stats = pl.pallas_call(
        attend_near_kernel,
        out_shape=(
            jax.ShapeDtypeStruct((rows, width), f32),
            jax.ShapeDtypeStruct((2, rows, width), f32),
        ),
        in_specs=[smem()] + [vmem()] * 4,
        out_specs=(vmem(), vmem()),
        compiler_params=params(),
        name="attend_near",
    )(place, queries, kv0, kv1, residual_in)
    kv2, held, stats = lax.optimization_barrier((kv2, held, stats))
    kvx2 = move(kv2, to_even)
    stream, home = pl.pallas_call(
        attend_far_kernel,
        out_shape=(
            jax.ShapeDtypeStruct((z_count, heads, 2, TILE, HEAD_DIM), bf16),
            jax.ShapeDtypeStruct((rows, width), bf16),
        ),
        in_specs=[smem()] + [vmem()] * 8,
        out_specs=(vmem(), vmem()),
        compiler_params=params(),
        name="attend_far",
    )(place, queries, kv2, kvx0, kvx1, kvx2, held, stats, residual_in)
    stream, first0, down1 = lax.optimization_barrier((stream, first0, down1))

    tiles = lax.all_to_all(
        stream.reshape(seq_count, TILE, HEAD_DIM), "seq", 0, 0, tiled=True
    )

    def pick(index, source):
        return pl.pallas_call(
            pick_kernel,
            out_shape=jax.ShapeDtypeStruct((index.shape[0], TILE, HEAD_DIM), bf16),
            in_specs=[smem(), vmem()],
            out_specs=vmem(),
            compiler_params=params(),
            name="pick",
        )(index, source)

    def same_core_exchange(x):
        x = x.reshape(chips, slots, TILE, HEAD_DIM)
        return lax.all_to_all(x, "seq", 0, 0, tiled=True, axis_index_groups=same_core)

    tiles, first0 = lax.optimization_barrier((tiles, first0))
    first1 = move(first0, swap)
    arrived = same_core_exchange(pick(block_of, tiles))
    arrived = arrived.reshape(z_count, heads, slots, TILE, HEAD_DIM)
    work = z_count * slots * TILE
    hid = first0.shape[2]
    parts = pl.pallas_call(
        project_kernel,
        out_shape=jax.ShapeDtypeStruct((tp_count, work + 2 * TILE, 2 * hid), bf16),
        in_specs=[vmem()] * 4,
        out_specs=vmem(),
        scratch_shapes=[pltpu.VMEM((work, width), bf16)],
        compiler_params=params(),
        name="project",
    )(arrived, gain, first0, first1)
    parts = lax.all_to_all(parts, "tp", 0, 0, tiled=True)

    def run_hidden(parts_ref, out_ref):
        hidden_kernel(width * tp_count, parts_ref, out_ref)

    hidden = pl.pallas_call(
        run_hidden,
        out_shape=jax.ShapeDtypeStruct((tp_count, work, hid), bf16),
        in_specs=[vmem()],
        out_specs=vmem(),
        compiler_params=params(),
        name="hidden",
    )(parts)
    hidden = lax.all_to_all(hidden, "tp", 0, 0, tiled=True)
    branch = pl.pallas_call(
        branch_kernel,
        out_shape=jax.ShapeDtypeStruct((z_count, heads, slots, TILE, HEAD_DIM), bf16),
        in_specs=[vmem(), vmem(), pl.BlockSpec(memory_space=pl.ANY)],
        out_specs=vmem(),
        scratch_shapes=[
            pltpu.VMEM((work, width), f32),
            pltpu.VMEM(down1.shape, bf16),
            pltpu.SemaphoreType.DMA,
        ],
        compiler_params=params(),
        name="branch",
    )(hidden, down0, down1)
    returned = same_core_exchange(branch).reshape(chips * slots, TILE, HEAD_DIM)
    finished = lax.all_to_all(pick(slot_of, returned), "seq", 0, 0, tiled=True)
    return pl.pallas_call(
        finish_kernel,
        out_shape=jax.ShapeDtypeStruct((rows, width), bf16),
        in_specs=[vmem()] * 2,
        out_specs=vmem(),
        compiler_params=params(),
        name="finish",
    )(home, finished.reshape(stream.shape))


def solution(mesh):
    in_specs = (
        P("seq", "tp"),
        P("seq", "tp"),
        P("seq", "tp"),
        P("seq", "tp"),
        P(),
        P(),
        P("seq", None, "tp"),
        P("seq", None, "tp"),
        P("seq", None, "tp"),
    )
    out_specs = P("seq", "tp")
    return jax.shard_map(local, mesh=mesh, in_specs=in_specs, out_specs=out_specs, check_vma=False)
```
